512 devices in a mesh: col: 16 (over y, core), row: 32 (over z, x).
Axes of the slice: x: 4, y: 8, z: 8, core: 2. Of those that a mesh axis runs over, the one named last changes fastest.
Arguments:
- pair_rep: float32 [512, 512, 128], P('row', 'col'), may hold values from -6 to 6
- cotangent: float32 [512, 512, 128], P('row', 'col'), may hold values from -6 to 6
- chain_ids: int32 [512], replicated, may hold values from 0 to 3, never falling along the last dimension, each value on 1 to 256 neighbouring positions
- template: int32 [8, 8], replicated, may hold values from 0 to 1
- norm_gain: float32 [128], replicated, may hold values from 0.25 to 1.75
- w_query: float32 [128, 128], replicated
- w_key: float32 [128, 128], replicated
- w_value: float32 [128, 128], replicated, may hold values from -0.5 to 0.5
- w_gate: float32 [128, 128], replicated, may hold values from -0.5 to 0.5
- gate_bias: float32 [128], replicated, may hold values from -4 to 4
- w_out: float32 [128, 128], replicated, may hold values from -0.5 to 0.5
- w_bias: float32 [4, 128], replicated, may hold values from -0.5 to 0.5
Outputs:
- update: float32 [512, 512, 128], P('row', 'col')
- grad_pair: float32 [512, 512, 128], P('row', 'col')
- grad_query: float32 [128, 128], replicated
- grad_key: float32 [128, 128], replicated
- grad_value: float32 [128, 128], replicated
- grad_gate: float32 [128, 128], replicated
- grad_gate_bias: float32 [128], replicated
- grad_out: float32 [128, 128], replicated
- grad_bias: float32 [4, 128], replicated
- grad_gain: float32 [128], replicated
The draws below stay inside these ranges and needn't reach their ends.
All inputs are finite; a program needn't handle non-finite values.
Results may differ from the reference program's by a relative error of at most 0.0003.
Values sent between devices are 32-bit elements; how exact they have to be, the bound alone decides.
No kernel may reach another device: no remote copies, remote signals or barrier semaphores. Data moves between devices by JAX's collectives and lax.ppermute only.
A program may use at most 64 MiB of HBM per device.

```python
import math
import jax
import jax.numpy as jnp
import numpy as np
from jax import lax

C = 128
H = 4
DH = 32
TOKENS = 512
NBLOCKS = 8
MBLOCK = 64
CHAINS = 4


def shared_projection(key):
    raw_values = jax.random.normal(key, (C, C), jnp.float32)
    return jnp.clip(raw_values, -4.0, 4.0) / jnp.sqrt(jnp.float32(C))


def draw_w_key(key, part):
    return shared_projection(key)


def draw_w_query(key, part):
    key = jax.random.fold_in(key, 7)
    own_values = jnp.clip(jax.random.normal(key, (C, C), jnp.float32), -4.0, 4.0) / jnp.sqrt(jnp.float32(C))
    return own_values


def draw_template(key, part):
    key = jax.random.fold_in(key, 5)
    tickets = jax.random.randint(key, (NBLOCKS, NBLOCKS), 0, 3 * NBLOCKS - 3)
    column_index = jnp.arange(NBLOCKS, dtype=jnp.int32)[None, :]
    return (tickets < NBLOCKS - 1 + column_index).astype(jnp.int32)


def block_scale(stream_key, shape, split, least, top_value):
    def one(position, shards_of):
        heights = jax.random.uniform(jax.random.fold_in(jax.random.fold_in(stream_key, 6), position), (shards_of,), jnp.float32, least / len(split), top_value / len(split))
        return jnp.repeat(jnp.exp(heights), shape[position] // shards_of).reshape((-1,) + (1,) * (len(shape) - position - 1))

    gain = one(*split[0])
    for cut in split[1:]:
        gain = gain * one(*cut)
    return gain


def split_up(number_of, total, most, skew):
    portions = [(1 << 20) // math.isqrt(rank ** skew) + 1 for rank in range(2, number_of + 1)]
    spare, given = total - most - (number_of - 1), [1] * (number_of - 1)
    while spare > 0:
        movable = [i for i in range(number_of - 1) if given[i] < most]
        pool, left = sum([portions[i] for i in movable]), spare
        for i in movable:
            more = min(most - given[i], max(1, left * portions[i] // pool), spare)
            given[i] = given[i] + more
            spare = spare - more
    return np.array([most] + given)


def uneven_parts(own_key, number_of, total, most, skew):
    if number_of == 2:
        one = jax.random.randint(own_key, (), max(1, total - most), min(most, total - 1) + 1)
        return jnp.stack([one, total - one])
    tallies = jnp.asarray(split_up(number_of, total, most, skew), jnp.int32)
    pairs = (number_of - 1) // 2
    giver, receiver = tallies[1:1 + 2 * pairs:2], tallies[2:2 + 2 * pairs:2]
    slack = jnp.minimum(giver - 1, most - receiver)
    moved = jax.random.randint(jax.random.fold_in(own_key, 1), (pairs,), 0, 1 << 20) % (slack + 1)
    tallies = tallies.at[1:1 + 2 * pairs:2].set(giver - moved).at[2:2 + 2 * pairs:2].set(receiver + moved)
    return tallies[jax.random.permutation(jax.random.fold_in(own_key, 2), number_of)]


def bell_draw(key, dims, width, reach, cuts=(), kind=jnp.bfloat16):
    array = width * jax.random.normal(key, dims, jnp.float32)
    if cuts:
        array = array * block_scale(key, dims, cuts, -0.22, 0.18)
    return jnp.clip(array, -reach, reach).astype(kind)


def setup_inputs(seed: int = 0) -> dict:
    streams_of = jax.random.split(jax.random.key(seed), 13)
    pair_rep = bell_draw(streams_of[0], (TOKENS, TOKENS, C), 1.0, 6.0, ((0, 32), (1, 16)), jnp.float32)
    cotangent = bell_draw(streams_of[1], (TOKENS, TOKENS, C), 1.0, 6.0, ((0, 32), (1, 16)), jnp.float32)
    chain_ids = jnp.searchsorted(jnp.cumsum(uneven_parts(streams_of[2], CHAINS, TOKENS, TOKENS // 2, 0)), jnp.arange(TOKENS), side="right").astype(jnp.int32)
    template = draw_template(jax.random.fold_in(streams_of[12], 71), 0)
    norm_gain = jnp.clip(1.0 + 0.15 * jax.random.normal(streams_of[4], (C,), jnp.float32), 0.25, 1.75)
    w_query = draw_w_query(jax.random.fold_in(streams_of[12], 71), 0)
    w_key = draw_w_key(jax.random.fold_in(streams_of[12], 71), 0)
    w_value = bell_draw(streams_of[7], (C, C), C ** -0.5, 0.5, (), jnp.float32)
    w_gate = bell_draw(streams_of[8], (C, C), C ** -0.5, 0.5, (), jnp.float32)
    gate_bias = bell_draw(streams_of[9], (C,), 1.0, 4.0, (), jnp.float32)
    w_out = bell_draw(streams_of[10], (C, C), C ** -0.5, 0.5, (), jnp.float32)
    w_bias = bell_draw(streams_of[11], (H, C), C ** -0.5, 0.5, (), jnp.float32)
    return {"pair_rep": pair_rep, "cotangent": cotangent, "chain_ids": chain_ids, "template": template, "norm_gain": norm_gain, "w_query": w_query, "w_key": w_key, "w_value": w_value, "w_gate": w_gate, "gate_bias": gate_bias, "w_out": w_out, "w_bias": w_bias}


HIGHEST = lax.Precision.HIGHEST

def layer_norm(cells, norm_gain):
    center = lax.optimization_barrier(jnp.mean(cells, axis=-1, keepdims=True))
    shifted = cells - center
    spread = lax.optimization_barrier(jnp.mean(shifted * shifted, axis=-1, keepdims=True))
    return shifted * lax.rsqrt(spread + 1e-05) * norm_gain

def column_attention(queries, keys_col, values_col, keep_col, bias_rows):
    scores = jnp.einsum('ihd,khd->ihk', queries, keys_col, precision=HIGHEST) * DH ** (-0.5) + bias_rows
    scores = jnp.where(keep_col[None, None, :] > 0, scores, -1000000000.0)
    highest = lax.stop_gradient(lax.optimization_barrier(jnp.max(scores, axis=2, keepdims=True)))
    weights = jnp.exp(scores - highest)
    normed_weights = weights / lax.optimization_barrier(jnp.sum(weights, axis=2, keepdims=True))
    return jnp.einsum('ihk,khd->ihd', normed_weights, values_col, precision=HIGHEST)

def triangle_update(pair_rep, norm_gain, w_query, w_key, w_value, w_gate, gate_bias, w_out, w_bias, keep_mask):
    normed = layer_norm(pair_rep, norm_gain)

    def project(weight):
        return jnp.einsum('ijc,cd->jid', normed, weight, precision=HIGHEST).reshape(TOKENS, TOKENS, H, DH)
    bias_rows = jnp.einsum('kic,hc->ihk', normed, w_bias, precision=HIGHEST)
    attend = jax.checkpoint(column_attention)
    attended = lax.map(lambda items: attend(items[0], items[1], items[2], items[3], bias_rows), (project(w_query), project(w_key), project(w_value), jnp.transpose(keep_mask)))
    attended = jnp.swapaxes(attended.reshape(TOKENS, TOKENS, C), 0, 1)
    gate = jax.nn.sigmoid(jnp.einsum('ijc,cd->ijd', normed, w_gate, precision=HIGHEST) + gate_bias)
    return jnp.einsum('ijc,cd->ijd', gate * attended, w_out, precision=HIGHEST)

def reference(pair_rep, cotangent, chain_ids, template, norm_gain, w_query, w_key, w_value, w_gate, gate_bias, w_out, w_bias):
    same_chain = (chain_ids[:, None] == chain_ids[None, :]).astype(jnp.int32)
    spread_mask = jnp.repeat(jnp.repeat(template, MBLOCK, axis=0), MBLOCK, axis=1)
    keep_mask = jnp.maximum(same_chain, spread_mask)

    def forward(pair_in, gain_in, query_in, key_in, value_in, gate_in, gate_bias_in, out_in, bias_in):
        return triangle_update(pair_in, gain_in, query_in, key_in, value_in, gate_in, gate_bias_in, out_in, bias_in, keep_mask)
    update, pullback = jax.vjp(forward, pair_rep, norm_gain, w_query, w_key, w_value, w_gate, gate_bias, w_out, w_bias)
    grads = pullback(cotangent)
    return (update, grads[0], grads[2] / TOKENS, grads[3] / TOKENS, grads[4] / TOKENS, grads[5] / TOKENS, grads[6] / TOKENS, grads[7] / TOKENS, grads[8] / TOKENS, grads[1] / TOKENS)
```

```python
import jax
import jax.numpy as jnp
from jax import lax
from jax.experimental import pallas as pl
from jax.experimental.pallas import tpu as pltpu
from jax.sharding import Mesh, PartitionSpec as P

F32 = jnp.float32
BF16 = jnp.bfloat16
NEG_FILL = -1000000000.0
ROWS = ("z", "x")
COLS = ("y", "core")
VMEM_BYTES = 48 * 1024 * 1024
NN = (((1,), (0,)), ((), ()))
NT = (((1,), (1,)), ((), ()))


def bdot(left, right, dims=NN):
    return lax.dot_general(left, right, dims, preferred_element_type=F32)


def split(value):
    high = value.astype(BF16)
    return high, (value - high.astype(F32)).astype(BF16)


def dot3(left, right, dims=NN):
    lh, ll = left if isinstance(left, tuple) else split(left)
    rh, rl = right if isinstance(right, tuple) else split(right)
    return bdot(lh, rh, dims) + (bdot(ll, rh, dims) + bdot(lh, rl, dims))


def lanes_of(shape):
    return lax.broadcasted_iota(jnp.int32, shape, 1)


def turn(value, amount):
    amount = amount % value.shape[1]
    return value if amount == 0 else pltpu.roll(value, amount, 1)


def head_weights(wq, wk, wv, wg, head, factor):
    lane = lanes_of(wq.shape)
    at = 32 * head
    out = jnp.where(lane < 32, turn(wq, -at) * factor, turn(wk, 32 - at))
    out = jnp.where(lane < 64, out, turn(wv, 64 - at))
    return jnp.where(lane < 96, out, turn(wg, 96 - at))


def project_kernel(
    factor, x_ref, cot_ref, gain_ref, wq_ref, wk_ref, wv_ref, wg_ref, gb_ref, wo_ref, wb_ref,
    send_ref, scaled_ref, inv_ref, gate_ref, dgated_ref,
):
    cells = jnp.swapaxes(x_ref[...], 0, 1).reshape(512, 128)
    cot = jnp.swapaxes(cot_ref[...], 0, 1).reshape(512, 128)
    center = jnp.mean(cells, axis=1, keepdims=True)
    shifted = cells - center
    spread = jnp.mean(shifted * shifted, axis=1, keepdims=True)
    inverse = lax.rsqrt(spread + 1e-05)
    scaled = shifted * inverse
    scaled_ref[...] = scaled
    inv_ref[...] = jnp.broadcast_to(inverse, (512, 128))
    normed = split(scaled * gain_ref[...])
    wq, wk, wv, wg = wq_ref[...], wk_ref[...], wv_ref[...], wg_ref[...]
    gate = jax.nn.sigmoid(dot3(normed, wg) + gb_ref[...])
    d_gated = dot3(cot, wo_ref[...], NT)
    gate_ref[...] = gate
    dgated_ref[...] = d_gated
    d_att = d_gated * gate
    bias = dot3(wb_ref[...], normed, NT)
    lane = lanes_of((512, 128))
    for head in range(4):
        weights = head_weights(wq, wk, wv, wg, head, factor)
        block = jnp.where(lane < 96, dot3(normed, weights), turn(d_att, 96 - 32 * head))
        send_ref[:, head, 0:64, :] = block.reshape(8, 64, 128)
        for part in range(4):
            row = bias[head : head + 1, part * 128 : (part + 1) * 128]
            send_ref[:, head, 64 + part, :] = jnp.broadcast_to(row, (8, 128))
        send_ref[:, head, 68:72, :] = jnp.zeros((8, 4, 128), F32)


def spread_lanes(value, group):
    lane = lanes_of(value.shape)
    kept = jnp.where((lane >= 32 * group) & (lane < 32 * group + 32), value, 0.0)
    kept = kept + pltpu.roll(kept, 32, 1)
    return kept + pltpu.roll(kept, 64, 1)


def parts_of(value):
    high = value.astype(BF16).astype(F32)
    return high, value - high


def attend_kernel(keep_ref, data_ref, bias_ref, out_ref, db_ref):
    column = pl.program_id(0)
    chunk = 256

    @pl.when(column == 0)
    def _():
        db_ref[...] = jnp.zeros_like(db_ref)

    data = data_ref[...].reshape(512, 128)
    lane = lanes_of((512, 128))
    odd = (lane // 32) % 2 == 1
    qh, ql = parts_of(spread_lanes(data, 0))
    kh, kl = parts_of(spread_lanes(data, 1))
    vh, vl = parts_of(spread_lanes(data, 2))
    q_left = jnp.where(odd, ql, qh)
    q_left16 = q_left.astype(BF16)
    k_right = jnp.where(lane < 64, kh, kl).astype(BF16)
    v_right = jnp.where(lane < 64, vh, vl).astype(BF16)
    k_first = jnp.where(lane < 32, kh, 0.0).astype(BF16)
    k_both = jnp.where(lane < 32, kh, jnp.where(lane < 64, kl, 0.0)).astype(BF16)
    v_first = jnp.where(lane >= 96, vh, 0.0).astype(BF16)
    v_both = jnp.where(lane >= 96, vh, jnp.where(lane >= 64, vl, 0.0)).astype(BF16)
    keep = keep_ref[pl.ds(column, 1), :] > 0
    dk_t = jnp.zeros((32, 512), F32)
    dv_t = jnp.zeros((32, 512), F32)
    heads = []
    for at in range(0, 512, chunk):
        rows = slice(at, at + chunk)
        pieces = [(core, y) for y in range(at // 64, (at + chunk) // 64) for core in range(2)]
        bias = jnp.concatenate([bias_ref[core, y] for core, y in pieces], axis=0)
        scores = bdot(q_left16[rows], k_right, NT) + bias
        scores = jnp.where(keep, scores, NEG_FILL)
        highest = jnp.max(scores, axis=1, keepdims=True)
        weights = jnp.exp(scores - highest)
        inv_total = 1.0 / jnp.sum(weights, axis=1, keepdims=True)
        wh, wl = split(weights)
        output = bdot(wh, v_both) + bdot(wl, v_first)
        sub = lanes_of((chunk, 128))
        output = (output + pltpu.roll(output, 32, 1)) * inv_total
        d_out = jnp.where(sub >= 96, data[rows], 0.0) * inv_total
        centred = jnp.sum(d_out * output, axis=1, keepdims=True)
        dh, dl = parts_of(spread_lanes(d_out, 3))
        d_left = jnp.where((sub // 32) % 2 == 1, dl, dh)
        d_scores = weights * (bdot(d_left.astype(BF16), v_right, NT) - centred)
        for place, (core, y) in enumerate(pieces):
            db_ref[core, y] += d_scores[place * 32 : (place + 1) * 32]
        sh, sl = split(d_scores)
        d_query = bdot(sh, k_both) + bdot(sl, k_first)
        d_query = d_query + pltpu.roll(d_query, 96, 1)
        heads.append(jnp.where(sub < 32, d_query, output))
        q_t = jnp.transpose(q_left[rows])[0:64].astype(BF16)
        d_t = jnp.transpose(d_left)[0:64].astype(BF16)
        both = bdot(q_t, sh)
        dk_t = dk_t + (both[0:32] + both[32:64] + bdot(q_t[0:32], sl))
        both = bdot(d_t, wh)
        dv_t = dv_t + (both[0:32] + both[32:64] + bdot(d_t[0:32], wl))
    zeros = jnp.zeros((32, 512), F32)
    turned = jnp.transpose(jnp.concatenate([zeros, dk_t, dv_t, zeros], axis=0))
    result = jnp.where(
        (lane >= 32) & (lane < 96), turned, jnp.concatenate(heads, axis=0)
    )
    out_ref[...] = result.reshape(32, 16, 128)


def block_kernel(
    factor, recv_ref, scaled_ref, gate_ref, dgated_ref, cot_ref, wq_ref, wk_ref, wv_ref, wg_ref, wo_ref,
    update_ref, dnorm_ref, param_ref, shift_ref,
):
    lane = lanes_of((512, 128))
    scaled = scaled_ref[...]
    gate = gate_ref[...]
    cot = jnp.swapaxes(cot_ref[...], 0, 1).reshape(512, 128)
    wq, wk, wv, wg = wq_ref[...], wk_ref[...], wv_ref[...], wg_ref[...]
    got = [recv_ref[:, head].reshape(512, 128) for head in range(4)]
    att = turn(got[3], 0)
    for head in range(3):
        moved = turn(got[head], 32 * head - 96)
        att = jnp.where((lane >= 32 * head) & (lane < 32 * head + 32), moved, att)
    gated = gate * att
    d_pre = dgated_ref[...] * att * gate * (1.0 - gate)
    shift_ref[...] = jnp.broadcast_to(jnp.sum(d_pre, axis=0, keepdims=True), (8, 128))
    update = dot3(gated, wo_ref[...])
    update_ref[...] = jnp.swapaxes(update.reshape(32, 16, 128), 0, 1)
    scaled_t = split(jnp.transpose(scaled))
    d_normed = jnp.zeros((512, 128), F32)
    for head in range(4):
        grads = split(jnp.where(lane < 96, got[head], turn(d_pre, 96 - 32 * head)))
        weights = head_weights(wq, wk, wv, wg, head, factor)
        d_normed = d_normed + dot3(grads, weights, NT)
        param_ref[head * 128 : (head + 1) * 128, :] = dot3(scaled_t, grads)
    param_ref[512:640, :] = dot3(jnp.transpose(gated), cot)
    dnorm_ref[...] = d_normed


def norm_kernel(
    recv_ref, dnorm_ref, scaled_ref, inv_ref, gain_ref, wb_ref, shift_ref, grad_ref, send_ref
):
    chunk = jnp.sum(recv_ref[:, 0:20, :], axis=0)
    rows = []
    for head in range(4):
        pieces = recv_ref[head, 20:24, :]
        for z in range(1, 8):
            pieces = pieces + recv_ref[z * 4 + head, 20:24, :]
        rows.append(jnp.concatenate([pieces[a : a + 1] for a in range(4)], axis=1))
    bias_t = jnp.concatenate(rows + [jnp.zeros((4, 512), F32)], axis=0)
    scaled = scaled_ref[...]
    wide = jnp.concatenate([bias_t, jnp.zeros((120, 512), F32)], axis=0)
    wb = jnp.concatenate([wb_ref[...], jnp.zeros((120, 128), F32)], axis=0)
    d_normed = dnorm_ref[...] + dot3(jnp.transpose(wide), wb)
    d_scaled = d_normed * gain_ref[...]
    mean_term = jnp.mean(d_scaled, axis=1, keepdims=True)
    cross_term = jnp.mean(d_scaled * scaled, axis=1, keepdims=True)
    d_input = inv_ref[...] * (d_scaled - mean_term - scaled * cross_term)
    grad_ref[...] = jnp.swapaxes(d_input.reshape(32, 16, 128), 0, 1)
    bias_w = dot3(bias_t, scaled)
    tail = jnp.concatenate(
        [chunk, bias_w[0:4], shift_ref[0:1], jnp.zeros((7, 128), F32)], axis=0
    )
    send_ref[...] = jnp.broadcast_to(tail[None], (16, 32, 128))


def share_kernel(recv_ref, send_ref):
    total = jnp.sum(recv_ref[...], axis=0)
    send_ref[...] = jnp.broadcast_to(total[None], (32, 32, 128))


def finish_kernel(
    factor, count, recv_ref, gain_ref, wq_ref, wk_ref, wv_ref, wg_ref, wb_ref,
    q_ref, k_ref, v_ref, g_ref, shift_ref, o_ref, b_ref, gain_out_ref, hold,
):
    for place in range(32):
        hold[place * 20 : (place + 1) * 20, :] = recv_ref[place, 0:20, :]
    rest = jnp.sum(recv_ref[:, 20:32, :], axis=0)
    wq, wk, wv, wg = wq_ref[...], wk_ref[...], wv_ref[...], wg_ref[...]
    lane = lanes_of((128, 128))
    gain_rows = jnp.transpose(jnp.broadcast_to(gain_ref[...], (128, 128)))
    blocks = [hold[head * 128 : (head + 1) * 128, :] for head in range(4)]
    scale = 1.0 / count
    gain_sum = jnp.zeros((128, 128), F32)
    for head in range(4):
        gain_sum = gain_sum + blocks[head] * head_weights(wq, wk, wv, wg, head, factor)
    for ref, group, times in ((q_ref, 0, factor), (k_ref, 1, 1.0), (v_ref, 2, 1.0), (g_ref, 3, 1.0)):
        full = turn(blocks[0], -32 * group)
        for head in range(1, 4):
            full = jnp.where(lane >= 32 * head, turn(blocks[head], 32 * (head - group)), full)
        ref[...] = full * gain_rows * (times * scale)
    o_ref[...] = hold[512:640, :] * scale
    b_ref[...] = rest[0:4] * gain_ref[...] * scale
    shift_ref[...] = rest[4:5] * scale
    gain_total = jnp.sum(jnp.transpose(gain_sum), axis=0, keepdims=True)
    gain_total = gain_total + jnp.sum(rest[0:4] * wb_ref[0:4], axis=0, keepdims=True)
    gain_out_ref[...] = gain_total * scale


def call(kernel, out_shape, name, **extra):
    return pl.pallas_call(
        kernel,
        out_shape=out_shape,
        name=name,
        compiler_params=pltpu.CompilerParams(vmem_limit_bytes=VMEM_BYTES),
        **extra,
    )


def shaped(*shape):
    return jax.ShapeDtypeStruct(shape, F32)


def swap(value, axes):
    return lax.all_to_all(value, axes, 0, 0, tiled=False)


def body(
    pair_rep, cotangent, chain_ids, template, norm_gain, w_query, w_key, w_value, w_gate, gate_bias, w_out, w_bias,
):
    factor = 32 ** (-0.5)
    tokens = chain_ids.shape[0]
    gain = norm_gain.reshape(1, 128)
    wb = jnp.concatenate([w_bias, jnp.zeros((4, 128), F32)], axis=0)

    send, scaled, inverse, gate, d_gated = call(
        lambda *refs: project_kernel(factor, *refs),
        [shaped(8, 4, 72, 128)] + [shaped(512, 128)] * 4,
        "project",
    )(pair_rep, cotangent, gain, w_query, w_key, w_value, w_gate, gate_bias.reshape(1, 128), w_out, wb)

    data = swap(send.reshape(32, 72, 128), ROWS)
    piece = data[:, 64:68, :].reshape(32, 32, 16)
    piece = jnp.transpose(piece, (1, 0, 2)).reshape(1, 32, 512)
    by_y = swap(jnp.broadcast_to(piece, (8, 32, 512)), "y")
    bias = swap(jnp.broadcast_to(by_y[None], (2, 8, 32, 512)), "core")

    first = (lax.axis_index("y") * 2 + lax.axis_index("core")) * 32 + lax.axis_index("z") * 4
    own_chain = lax.dynamic_slice_in_dim(chain_ids, first, 4, 0)
    own_block = lax.dynamic_slice_in_dim(template, first // 64, 1, 1)
    block_keep = jnp.broadcast_to(own_block, (8, 64)).reshape(1, 512) > 0
    keep = ((own_chain[:, None] == chain_ids[None, :]) | block_keep).astype(jnp.int32)

    back, d_bias = pl.pallas_call(
        attend_kernel,
        grid=(4,),
        in_specs=[
            pl.BlockSpec((4, 512), lambda j: (0, 0)),
            pl.BlockSpec((32, 16, 128), lambda j: (0, j, 0)),
            pl.BlockSpec((2, 8, 32, 512), lambda j: (0, 0, 0, 0)),
        ],
        out_specs=[
            pl.BlockSpec((32, 16, 128), lambda j: (0, j, 0)),
            pl.BlockSpec((2, 8, 32, 512), lambda j: (0, 0, 0, 0)),
        ],
        out_shape=[shaped(32, 64, 128), shaped(2, 8, 32, 512)],
        name="attend",
        compiler_params=pltpu.CompilerParams(vmem_limit_bytes=VMEM_BYTES),
    )(keep, data, bias)

    got = swap(back, ROWS)
    d_bias = jnp.sum(swap(d_bias, "core"), axis=0)
    d_bias = jnp.sum(swap(d_bias, "y"), axis=0)
    d_bias = jnp.transpose(d_bias.reshape(32, 32, 16), (1, 0, 2)).reshape(32, 4, 128)

    update, d_normed, params, d_shift = call(
        lambda *refs: block_kernel(factor, *refs),
        [shaped(16, 32, 128), shaped(512, 128), shaped(640, 128), shaped(8, 128)],
        "block_grads",
    )(got.reshape(8, 4, 64, 128), scaled, gate, d_gated, cotangent, w_query, w_key, w_value, w_gate, w_out)

    small = swap(jnp.concatenate([params.reshape(32, 20, 128), d_bias], axis=1), ROWS)
    grad_pair, tail = call(norm_kernel, [shaped(16, 32, 128), shaped(16, 32, 128)], "norm_back")(
        small, d_normed, scaled, inverse, gain, wb, d_shift
    )
    tail = swap(tail, COLS)
    tail = call(share_kernel, shaped(32, 32, 128), "share")(tail)
    tail = swap(tail, ROWS)
    square = shaped(128, 128)
    grads = call(
        lambda *refs: finish_kernel(factor, float(tokens), *refs),
        [square, square, square, square, shaped(1, 128), square, shaped(4, 128), shaped(1, 128)],
        "finish",
        scratch_shapes=[pltpu.VMEM((640, 128), F32)],
    )(tail, gain, w_query, w_key, w_value, w_gate, wb)
    gq, gk, gv, gg, gshift, go, gb, ggain = grads
    return update, grad_pair, gq, gk, gv, gg, gshift.reshape(128), go, gb, ggain.reshape(128)


def solution(mesh):
    fine = Mesh(mesh.devices.reshape(8, 2, 8, 4), ("y", "core", "z", "x"))
    block = P(ROWS, COLS, None)
    return jax.shard_map(
        body,
        mesh=fine,
        in_specs=(block, block) + (P(),) * 10,
        out_specs=(block, block) + (P(),) * 8,
        check_vma=False,
    )
```

```python
import jax
import jax.numpy as jnp
from jax import lax
from jax.experimental import pallas as pl
from jax.experimental.pallas import tpu as pltpu
from jax.sharding import Mesh, PartitionSpec as P

F32 = jnp.float32
BF16 = jnp.bfloat16
NEG_FILL = -1000000000.0
ROWS = ("z", "x")
COLS = ("y", "core")
VMEM_BYTES = 48 * 1024 * 1024
NN = (((1,), (0,)), ((), ()))
NT = (((1,), (1,)), ((), ()))


def bdot(left, right, dims=NN):
    return lax.dot_general(left, right, dims, preferred_element_type=F32)


def split(value):
    high = value.astype(BF16)
    return high, (value - high.astype(F32)).astype(BF16)


def dot3(left, right, dims=NN):
    lh, ll = left if isinstance(left, tuple) else split(left)
    rh, rl = right if isinstance(right, tuple) else split(right)
    return bdot(lh, rh, dims) + (bdot(ll, rh, dims) + bdot(lh, rl, dims))


def lanes_of(shape):
    return lax.broadcasted_iota(jnp.int32, shape, 1)


def turn(value, amount):
    amount = amount % value.shape[1]
    return value if amount == 0 else pltpu.roll(value, amount, 1)


def head_weights(wq, wk, wv, wg, head, factor):
    lane = lanes_of(wq.shape)
    at = 32 * head
    out = jnp.where(lane < 32, turn(wq, -at) * factor, turn(wk, 32 - at))
    out = jnp.where(lane < 64, out, turn(wv, 64 - at))
    return jnp.where(lane < 96, out, turn(wg, 96 - at))


def project_kernel(
    factor, x_in, cot_in, gain_in, wq_in, wk_in, wv_in, wg_in, gb_in, wo_in, wb_in,
    send_ref, piece_ref, scaled_ref, inv_ref, gate_ref, dgated_ref,
    x_ref, cot_ref, gain_ref, wq_ref, wk_ref, wv_ref, wg_ref, gb_ref, wo_ref, wb_ref, sems,
):
    sources = (x_in, gain_in, wb_in, wq_in, wk_in, wv_in, wg_in, gb_in, cot_in, wo_in)
    targets = (x_ref, gain_ref, wb_ref, wq_ref, wk_ref, wv_ref, wg_ref, gb_ref, cot_ref, wo_ref)
    copies = [
        pltpu.make_async_copy(source, target, sems.at[place])
        for place, (source, target) in enumerate(zip(sources, targets))
    ]
    for copy in copies:
        copy.start()
    for copy in copies:
        copy.wait()
    cells = jnp.swapaxes(x_ref[...], 0, 1).reshape(512, 128)
    cot = jnp.swapaxes(cot_ref[...], 0, 1).reshape(512, 128)
    center = jnp.mean(cells, axis=1, keepdims=True)
    shifted = cells - center
    spread = jnp.mean(shifted * shifted, axis=1, keepdims=True)
    inverse = lax.rsqrt(spread + 1e-05)
    scaled = shifted * inverse
    scaled_ref[...] = scaled
    inv_ref[...] = jnp.broadcast_to(inverse, (512, 128))
    normed = split(scaled * gain_ref[...])
    wq, wk, wv, wg = wq_ref[...], wk_ref[...], wv_ref[...], wg_ref[...]
    gate = jax.nn.sigmoid(dot3(normed, wg) + gb_ref[...])
    d_gated = dot3(cot, wo_ref[...], NT)
    gate_ref[...] = gate
    dgated_ref[...] = d_gated
    d_att = d_gated * gate
    wb = jnp.concatenate([wb_ref[...], jnp.zeros((4, 128), F32)], axis=0)
    bias = dot3(wb, normed, NT)
    lane = lanes_of((512, 128))
    for head in range(4):
        weights = head_weights(wq, wk, wv, wg, head, factor)
        block = jnp.where(lane < 96, dot3(normed, weights), turn(d_att, 96 - 32 * head))
        send_ref[:, head] = block.reshape(8, 64, 128)
        for part in range(4):
            row = bias[head : head + 1, part * 128 : (part + 1) * 128]
            piece_ref[:, head, part, :] = jnp.broadcast_to(row, (8, 128))


def spread_lanes(value, group):
    lane = lanes_of(value.shape)
    kept = jnp.where((lane >= 32 * group) & (lane < 32 * group + 32), value, 0.0)
    kept = kept + pltpu.roll(kept, 32, 1)
    return kept + pltpu.roll(kept, 64, 1)


def parts_of(value):
    high = value.astype(BF16).astype(F32)
    return high, value - high


def attend_kernel(place_ref, keep_ref, data_ref, own_ref, other_ref, out_ref, d_own_ref, d_other_ref):
    column = pl.program_id(0)
    y, core = place_ref[0], place_ref[1]

    @pl.when(column == 0)
    def _():
        d_own_ref[...] = jnp.zeros_like(d_own_ref)
        d_other_ref[...] = jnp.zeros_like(d_other_ref)

    data = data_ref[...].reshape(512, 128)
    lane = lanes_of((512, 128))
    kh, kl = parts_of(spread_lanes(data, 1))
    vh, vl = parts_of(spread_lanes(data, 2))
    k_right = jnp.where(lane < 64, kh, kl).astype(BF16)
    v_right = jnp.where(lane < 64, vh, vl).astype(BF16)
    k_first = jnp.where(lane < 32, kh, 0.0).astype(BF16)
    k_both = jnp.where(lane < 32, kh, jnp.where(lane < 64, kl, 0.0)).astype(BF16)
    v_first = jnp.where(lane >= 96, vh, 0.0).astype(BF16)
    v_both = jnp.where(lane >= 96, vh, jnp.where(lane >= 64, vl, 0.0)).astype(BF16)
    keep = keep_ref[pl.ds(column, 1), :] > 0
    sub = lanes_of((256, 128))
    odd = (sub // 32) % 2 == 1
    turned = []
    halves = []
    for side, (bias_ref, db_ref) in enumerate(((own_ref, d_own_ref), (other_ref, d_other_ref))):
        half = core if side == 0 else 1 - core
        starts = [(y ^ ((s >> 2) | (s & 2) | ((s & 1) << 2))) * 4 + half * 2 for s in range(8)]
        rows = jnp.concatenate([data_ref[pl.ds(start, 2)].reshape(32, 128) for start in starts], axis=0)
        qh, ql = parts_of(spread_lanes(rows, 0))
        q_left = jnp.where(odd, ql, qh)
        scores = bdot(q_left.astype(BF16), k_right, NT) + bias_ref[...].reshape(256, 512)
        scores = jnp.where(keep, scores, NEG_FILL)
        highest = jnp.max(scores, axis=1, keepdims=True)
        weights = jnp.exp(scores - highest)
        inv_total = 1.0 / jnp.sum(weights, axis=1, keepdims=True)
        wh, wl = split(weights)
        output = bdot(wh, v_both) + bdot(wl, v_first)
        output = (output + pltpu.roll(output, 32, 1)) * inv_total
        d_out = jnp.where(sub >= 96, rows, 0.0) * inv_total
        centred = jnp.sum(d_out * output, axis=1, keepdims=True)
        dh, dl = parts_of(spread_lanes(d_out, 3))
        d_left = jnp.where(odd, dl, dh)
        d_scores = weights * (bdot(d_left.astype(BF16), v_right, NT) - centred)
        db_ref[...] += d_scores.reshape(8, 32, 512)
        sh, sl = split(d_scores)
        d_query = bdot(sh, k_both) + bdot(sl, k_first)
        d_query = d_query + pltpu.roll(d_query, 96, 1)
        halves.append((starts, jnp.where(sub < 32, d_query, output)))
        q_t = jnp.transpose(q_left)[0:64].astype(BF16)
        d_t = jnp.transpose(d_left)[0:64].astype(BF16)
        both = bdot(q_t, sh)
        dk_t = both[0:32] + both[32:64] + bdot(q_t[0:32], sl)
        both = bdot(d_t, wh)
        dv_t = both[0:32] + both[32:64] + bdot(d_t[0:32], wl)
        turned.append((dk_t, dv_t))
    zeros = jnp.zeros((32, 512), F32)
    dk_t = turned[0][0] + turned[1][0]
    dv_t = turned[0][1] + turned[1][1]
    result = jnp.transpose(jnp.concatenate([zeros, dk_t, dv_t, zeros], axis=0))
    out_ref[...] = result.reshape(32, 16, 128)
    mixed = (sub >= 32) & (sub < 96)
    for starts, value in halves:
        held = jnp.concatenate([out_ref[pl.ds(start, 2)].reshape(32, 128) for start in starts], axis=0)
        value = jnp.where(mixed, held, value)
        for s, start in enumerate(starts):
            out_ref[pl.ds(start, 2)] = value[s * 32 : (s + 1) * 32].reshape(2, 16, 128)


def block_kernel(
    factor, recv_ref, scaled_ref, gate_ref, dgated_ref, cot_ref, wq_ref, wk_ref, wv_ref, wg_ref, wo_ref,
    update_ref, dnorm_ref, param_ref,
):
    lane = lanes_of((512, 128))
    scaled = scaled_ref[...]
    gate = gate_ref[...]
    cot = jnp.swapaxes(cot_ref[...], 0, 1).reshape(512, 128)
    wq, wk, wv, wg = wq_ref[...], wk_ref[...], wv_ref[...], wg_ref[...]
    got = [recv_ref[:, head].reshape(512, 128) for head in range(4)]
    att = turn(got[3], 0)
    for head in range(3):
        moved = turn(got[head], 32 * head - 96)
        att = jnp.where((lane >= 32 * head) & (lane < 32 * head + 32), moved, att)
    gated = gate * att
    d_pre = dgated_ref[...] * att * gate * (1.0 - gate)
    update = dot3(gated, wo_ref[...])
    update_ref[...] = jnp.swapaxes(update.reshape(32, 16, 128), 0, 1)
    scaled_t = split(jnp.transpose(jnp.where(lane == 127, 1.0, scaled)))
    d_normed = jnp.zeros((512, 128), F32)
    for head in range(4):
        grads = split(jnp.where(lane < 96, got[head], turn(d_pre, 96 - 32 * head)))
        weights = head_weights(wq, wk, wv, wg, head, factor)
        d_normed = d_normed + dot3(grads, weights, NT)
        param_ref[head * 128 : (head + 1) * 128, :] = dot3(scaled_t, grads)
    param_ref[512:640, :] = dot3(jnp.transpose(gated), cot)
    dnorm_ref[...] = d_normed


def norm_kernel(
    recv_ref, dnorm_ref, scaled_ref, inv_ref, gain_ref, wb_ref, grad_ref, send_ref
):
    chunk = jnp.sum(recv_ref[:, 0:20, :], axis=0)
    rows = []
    for head in range(4):
        pieces = recv_ref[head, 20:24, :]
        for z in range(1, 8):
            pieces = pieces + recv_ref[z * 4 + head, 20:24, :]
        rows.append(jnp.concatenate([pieces[a : a + 1] for a in range(4)], axis=1))
    bias_t = jnp.concatenate(rows + [jnp.zeros((4, 512), F32)], axis=0)
    scaled = scaled_ref[...]
    wide = jnp.concatenate([bias_t, jnp.zeros((120, 512), F32)], axis=0)
    wb = jnp.concatenate([wb_ref[...], jnp.zeros((124, 128), F32)], axis=0)
    d_normed = dnorm_ref[...] + dot3(jnp.transpose(wide), wb)
    d_scaled = d_normed * gain_ref[...]
    mean_term = jnp.mean(d_scaled, axis=1, keepdims=True)
    cross_term = jnp.mean(d_scaled * scaled, axis=1, keepdims=True)
    d_input = inv_ref[...] * (d_scaled - mean_term - scaled * cross_term)
    grad_ref[...] = jnp.swapaxes(d_input.reshape(32, 16, 128), 0, 1)
    bias_w = dot3(bias_t, scaled)
    tail = jnp.concatenate([chunk, bias_w[0:4]], axis=0)
    send_ref[...] = jnp.broadcast_to(tail[None], (16, 24, 128))


def share_kernel(recv_ref, send_ref):
    total = jnp.sum(recv_ref[...], axis=0)
    send_ref[...] = jnp.broadcast_to(total[None], (32, 24, 128))


def finish_kernel(
    factor, count, recv_ref, gain_ref, wq_ref, wk_ref, wv_ref, wg_ref, wb_ref,
    q_ref, k_ref, v_ref, g_ref, shift_ref, o_ref, b_ref, gain_out_ref, hold,
):
    for place in range(32):
        hold[place * 20 : (place + 1) * 20, :] = recv_ref[place, 0:20, :]
    bias_w = jnp.sum(recv_ref[:, 20:24, :], axis=0)
    wq, wk, wv, wg = wq_ref[...], wk_ref[...], wv_ref[...], wg_ref[...]
    lane = lanes_of((128, 128))
    gain_rows = jnp.transpose(jnp.broadcast_to(gain_ref[...], (128, 128)))
    last = lax.broadcasted_iota(jnp.int32, (128, 128), 0) == 127
    scale = 1.0 / count
    blocks = []
    shift = jnp.zeros((1, 128), F32)
    for head in range(4):
        block = hold[head * 128 : (head + 1) * 128, :]
        sums = turn(block[127:128], 32 * head - 96)
        shift = jnp.where((lane[0:1] >= 32 * head) & (lane[0:1] < 32 * head + 32), sums, shift)
        block = jnp.where(last, 0.0, block)
        blocks.append(jnp.where(last, -jnp.sum(block, axis=0, keepdims=True), block))
    gain_sum = jnp.zeros((128, 128), F32)
    for head in range(4):
        gain_sum = gain_sum + blocks[head] * head_weights(wq, wk, wv, wg, head, factor)
    for ref, group, times in ((q_ref, 0, factor), (k_ref, 1, 1.0), (v_ref, 2, 1.0), (g_ref, 3, 1.0)):
        full = turn(blocks[0], -32 * group)
        for head in range(1, 4):
            full = jnp.where(lane >= 32 * head, turn(blocks[head], 32 * (head - group)), full)
        ref[...] = full * gain_rows * (times * scale)
    o_ref[...] = hold[512:640, :] * scale
    b_ref[...] = bias_w * gain_ref[...] * scale
    shift_ref[...] = shift * scale
    gain_total = jnp.sum(jnp.transpose(gain_sum), axis=0, keepdims=True)
    gain_total = gain_total + jnp.sum(bias_w * wb_ref[...], axis=0, keepdims=True)
    gain_out_ref[...] = gain_total * scale


def call(kernel, out_shape, name, **extra):
    return pl.pallas_call(
        kernel,
        out_shape=out_shape,
        name=name,
        compiler_params=pltpu.CompilerParams(vmem_limit_bytes=VMEM_BYTES),
        **extra,
    )


def shaped(*shape):
    return jax.ShapeDtypeStruct(shape, F32)


def swap(value, axes):
    return lax.all_to_all(value, axes, 0, 0, tiled=False)


def partner(value, axis, flip):
    return lax.ppermute(value, axis, [(at, at ^ flip) for at in range(lax.axis_size(axis))])


def body(
    pair_rep, cotangent, chain_ids, template, norm_gain, w_query, w_key, w_value, w_gate, gate_bias, w_out, w_bias,
):
    factor = 32 ** (-0.5)
    tokens = chain_ids.shape[0]
    gain = norm_gain.reshape(1, 128)
    square = shaped(128, 128)
    row = shaped(1, 128)
    here = [shaped(16, 32, 128)] * 2 + [row] + [square] * 4 + [row, square, shaped(4, 128)]

    send, piece, scaled, inverse, gate, d_gated = call(
        lambda *refs: project_kernel(factor, *refs),
        [shaped(8, 4, 64, 128), shaped(8, 4, 4, 128)] + [shaped(512, 128)] * 4,
        "project",
        in_specs=[pl.BlockSpec(memory_space=pltpu.HBM)] * 10,
        scratch_shapes=[pltpu.VMEM(part.shape, F32) for part in here] + [pltpu.SemaphoreType.DMA((10,))],
    )(pair_rep, cotangent, gain, w_query, w_key, w_value, w_gate, gate_bias.reshape(1, 128), w_out, w_bias)

    piece = swap(piece.reshape(32, 4, 128), ROWS)
    piece, send = lax.optimization_barrier((piece, send))
    data = swap(send.reshape(32, 64, 128), ROWS)
    own = jnp.transpose(piece.reshape(32, 32, 16), (1, 0, 2)).reshape(1, 32, 512)
    for flip in (4, 2, 1):
        own = jnp.concatenate([own, partner(own, "y", flip)], axis=0)
    other = partner(own, "core", 1)

    y, core = lax.axis_index("y"), lax.axis_index("core")
    first = (y * 2 + core) * 32 + lax.axis_index("z") * 4
    own_chain = lax.dynamic_slice_in_dim(chain_ids, first, 4, 0)
    own_block = lax.dynamic_slice_in_dim(template, first // 64, 1, 1)
    block_keep = jnp.broadcast_to(own_block, (8, 64)).reshape(1, 512) > 0
    keep = ((own_chain[:, None] == chain_ids[None, :]) | block_keep).astype(jnp.int32)

    columns = pl.BlockSpec((32, 16, 128), lambda j: (0, j, 0))
    slots = pl.BlockSpec((8, 32, 512), lambda j: (0, 0, 0))
    back, d_own, d_other = pl.pallas_call(
        attend_kernel,
        grid=(4,),
        in_specs=[
            pl.BlockSpec(memory_space=pltpu.SMEM),
            pl.BlockSpec((4, 512), lambda j: (0, 0)),
            columns,
            slots,
            slots,
        ],
        out_specs=[columns, slots, slots],
        out_shape=[shaped(32, 64, 128), shaped(8, 32, 512), shaped(8, 32, 512)],
        name="attend",
        compiler_params=pltpu.CompilerParams(vmem_limit_bytes=VMEM_BYTES),
    )(jnp.stack([y, core]).astype(jnp.int32), keep, data, own, other)

    got = swap(back, ROWS)
    d_bias = d_own + partner(d_other, "core", 1)
    for flip in (1, 2, 4):
        half = d_bias.shape[0] // 2
        d_bias = d_bias[:half] + partner(d_bias[half:], "y", flip)
    d_bias = jnp.transpose(d_bias.reshape(32, 32, 16), (1, 0, 2)).reshape(32, 4, 128)

    update, d_normed, params = call(
        lambda *refs: block_kernel(factor, *refs),
        [shaped(16, 32, 128), shaped(512, 128), shaped(640, 128)],
        "block_grads",
    )(got.reshape(8, 4, 64, 128), scaled, gate, d_gated, cotangent, w_query, w_key, w_value, w_gate, w_out)

    small = swap(jnp.concatenate([params.reshape(32, 20, 128), d_bias], axis=1), ROWS)
    grad_pair, tail = call(norm_kernel, [shaped(16, 32, 128), shaped(16, 24, 128)], "norm_back")(
        small, d_normed, scaled, inverse, gain, w_bias
    )
    tail = swap(tail, COLS)
    tail = call(share_kernel, shaped(32, 24, 128), "share")(tail)
    tail = swap(tail, ROWS)
    grads = call(
        lambda *refs: finish_kernel(factor, float(tokens), *refs),
        [square, square, square, square, row, square, shaped(4, 128), row],
        "finish",
        scratch_shapes=[pltpu.VMEM((640, 128), F32)],
    )(tail, gain, w_query, w_key, w_value, w_gate, w_bias)
    gq, gk, gv, gg, gshift, go, gb, ggain = grads
    return update, grad_pair, gq, gk, gv, gg, gshift.reshape(128), go, gb, ggain.reshape(128)


def solution(mesh):
    fine = Mesh(mesh.devices.reshape(8, 2, 8, 4), ("y", "core", "z", "x"))
    block = P(ROWS, COLS, None)
    return jax.shard_map(
        body,
        mesh=fine,
        in_specs=(block, block) + (P(),) * 10,
        out_specs=(block, block) + (P(),) * 8,
        check_vma=False,
    )
```

```python
import jax
import jax.numpy as jnp
from jax import lax
from jax.experimental import pallas as pl
from jax.experimental.pallas import tpu as pltpu
from jax.sharding import Mesh, PartitionSpec as P

F32 = jnp.float32
BF16 = jnp.bfloat16
NEG_FILL = -1000000000.0
ROWS = ("z", "x")
COLS = ("y", "core")
VMEM_BYTES = 48 * 1024 * 1024
NN = (((1,), (0,)), ((), ()))
NT = (((1,), (1,)), ((), ()))


def bdot(left, right, dims=NN):
    return lax.dot_general(left, right, dims, preferred_element_type=F32)


def split(value):
    high = value.astype(BF16)
    return high, (value - high.astype(F32)).astype(BF16)


def dot3(left, right, dims=NN):
    lh, ll = left if isinstance(left, tuple) else split(left)
    rh, rl = right if isinstance(right, tuple) else split(right)
    return bdot(lh, rh, dims) + (bdot(ll, rh, dims) + bdot(lh, rl, dims))


def lanes_of(shape):
    return lax.broadcasted_iota(jnp.int32, shape, 1)


def turn(value, amount):
    amount = amount % value.shape[1]
    return value if amount == 0 else pltpu.roll(value, amount, 1)


def head_weights(wq, wk, wv, wg, head, factor):
    lane = lanes_of(wq.shape)
    at = 32 * head
    out = jnp.where(lane < 32, turn(wq, -at) * factor, turn(wk, 32 - at))
    out = jnp.where(lane < 64, out, turn(wv, 64 - at))
    return jnp.where(lane < 96, out, turn(wg, 96 - at))


def norm_kernel(x_ref, gain_ref, wb_ref, piece_ref, scaled_ref, inv_ref):
    cells = jnp.swapaxes(x_ref[...], 0, 1).reshape(512, 128)
    center = jnp.mean(cells, axis=1, keepdims=True)
    shifted = cells - center
    spread = jnp.mean(shifted * shifted, axis=1, keepdims=True)
    inverse = lax.rsqrt(spread + 1e-05)
    scaled = shifted * inverse
    scaled_ref[...] = scaled
    inv_ref[...] = jnp.broadcast_to(inverse, (512, 128))
    wb = jnp.concatenate([wb_ref[...], jnp.zeros((4, 128), F32)], axis=0)
    bias = dot3(wb, scaled * gain_ref[...], NT)
    for head in range(4):
        for part in range(4):
            row = bias[head : head + 1, part * 128 : (part + 1) * 128]
            piece_ref[:, head, part, :] = jnp.broadcast_to(row, (8, 128))


def project_kernel(
    factor, place_ref, scaled_ref, cot_ref, gain_ref, wq_ref, wk_ref, wv_ref, wg_ref, gb_ref, wo_ref,
    chain_ref, template_ref, send_ref, gate_ref, dgated_ref, keep_ref,
):
    cot = jnp.swapaxes(cot_ref[...], 0, 1).reshape(512, 128)
    normed = split(scaled_ref[...] * gain_ref[...])
    wq, wk, wv, wg = wq_ref[...], wk_ref[...], wv_ref[...], wg_ref[...]
    gate = jax.nn.sigmoid(dot3(normed, wg) + gb_ref[...])
    d_gated = dot3(cot, wo_ref[...], NT)
    gate_ref[...] = gate
    dgated_ref[...] = d_gated
    d_att = d_gated * gate
    lane = lanes_of((512, 128))
    for head in range(4):
        weights = head_weights(wq, wk, wv, wg, head, factor)
        block = jnp.where(lane < 96, dot3(normed, weights), turn(d_att, 96 - 32 * head))
        send_ref[:, head] = block.reshape(8, 64, 128)
    first = place_ref[2]
    chain = chain_ref[...]
    token = lanes_of((1, 512))
    near = lanes_of((8, 8)) == first // 64
    blocks = jnp.max(jnp.where(near, template_ref[...], 0), axis=1, keepdims=True)
    open_block = jnp.zeros((1, 512), jnp.int32)
    for block in range(8):
        open_block = jnp.where(token // 64 == block, blocks[block : block + 1], open_block)
    for column in range(4):
        own = jnp.max(jnp.where(token == first + column, chain, 0), axis=1, keepdims=True)
        keep_ref[column : column + 1, :] = jnp.where(chain == own, 1, open_block)


def spread_lanes(value, group):
    lane = lanes_of(value.shape)
    kept = jnp.where((lane >= 32 * group) & (lane < 32 * group + 32), value, 0.0)
    kept = kept + pltpu.roll(kept, 32, 1)
    return kept + pltpu.roll(kept, 64, 1)


def parts_of(value):
    high = value.astype(BF16).astype(F32)
    return high, value - high


def attend_kernel(place_ref, keep_ref, data_ref, own_ref, other_ref, out_ref, d_own_ref, d_other_ref):
    column = pl.program_id(0)
    y, core = place_ref[0], place_ref[1]

    @pl.when(column == 0)
    def _():
        d_own_ref[...] = jnp.zeros_like(d_own_ref)
        d_other_ref[...] = jnp.zeros_like(d_other_ref)

    data = data_ref[...].reshape(512, 128)
    lane = lanes_of((512, 128))
    kh, kl = parts_of(spread_lanes(data, 1))
    vh, vl = parts_of(spread_lanes(data, 2))
    k_right = jnp.where(lane < 64, kh, kl).astype(BF16)
    v_right = jnp.where(lane < 64, vh, vl).astype(BF16)
    k_first = jnp.where(lane < 32, kh, 0.0).astype(BF16)
    k_both = jnp.where(lane < 32, kh, jnp.where(lane < 64, kl, 0.0)).astype(BF16)
    v_first = jnp.where(lane >= 96, vh, 0.0).astype(BF16)
    v_both = jnp.where(lane >= 96, vh, jnp.where(lane >= 64, vl, 0.0)).astype(BF16)
    keep = keep_ref[pl.ds(column, 1), :] > 0
    chunk_rows = 256
    per = chunk_rows // 32
    sub = lanes_of((chunk_rows, 128))
    odd = (sub // 32) % 2 == 1
    chunks = []
    for side, (bias_ref, db_ref) in enumerate(((own_ref, d_own_ref), (other_ref, d_other_ref))):
        half = core if side == 0 else 1 - core
        for s0 in range(0, 8, per):
            starts = [(y ^ ((s >> 2) | (s & 2) | ((s & 1) << 2))) * 4 + half * 2 for s in range(s0, s0 + per)]
            chunks.append((starts, bias_ref, db_ref, s0))

    def first(chunk):
        starts, bias_ref, db_ref, s0 = chunk
        rows = jnp.concatenate([data_ref[pl.ds(start, 2)].reshape(32, 128) for start in starts], axis=0)
        qh, ql = parts_of(spread_lanes(rows, 0))
        q_left = jnp.where(odd, ql, qh)
        scores = bdot(q_left.astype(BF16), k_right, NT) + bias_ref[s0 : s0 + per].reshape(chunk_rows, 512)
        return rows, q_left, jnp.where(keep, scores, NEG_FILL)

    def second(state):
        rows, q_left, scores = state
        highest = jnp.max(scores, axis=1, keepdims=True)
        weights = jnp.exp(scores - highest)
        inv_total = 1.0 / jnp.sum(weights, axis=1, keepdims=True)
        wh, wl = split(weights)
        output = bdot(wh, v_both) + bdot(wl, v_first)
        output = (output + pltpu.roll(output, 32, 1)) * inv_total
        d_out = jnp.where(sub >= 96, rows, 0.0) * inv_total
        centred = jnp.sum(d_out * output, axis=1, keepdims=True)
        dh, dl = parts_of(spread_lanes(d_out, 3))
        d_left = jnp.where(odd, dl, dh)
        d_weights = bdot(d_left.astype(BF16), v_right, NT)
        d_t = jnp.transpose(d_left)[0:64].astype(BF16)
        both = bdot(d_t, wh)
        dv_t = both[0:32] + both[32:64] + bdot(d_t[0:32], wl)
        return weights, output, d_weights, centred, dv_t, q_left

    def third(chunk, state):
        starts, bias_ref, db_ref, s0 = chunk
        weights, output, d_weights, centred, dv_t, q_left = state
        d_scores = weights * (d_weights - centred)
        db_ref[s0 : s0 + per] += d_scores.reshape(per, 32, 512)
        sh, sl = split(d_scores)
        d_query = bdot(sh, k_both) + bdot(sl, k_first)
        d_query = d_query + pltpu.roll(d_query, 96, 1)
        q_t = jnp.transpose(q_left)[0:64].astype(BF16)
        both = bdot(q_t, sh)
        dk_t = both[0:32] + both[32:64] + bdot(q_t[0:32], sl)
        return jnp.where(sub < 32, d_query, output), dk_t, dv_t

    n = len(chunks)
    ones, twos, dones = {}, {}, {}
    for step in range(n + 2):
        if step < n:
            ones[step] = first(chunks[step])
        if 0 <= step - 1 < n:
            twos[step - 1] = second(ones.pop(step - 1))
        if 0 <= step - 2 < n:
            dones[step - 2] = third(chunks[step - 2], twos.pop(step - 2))
    zeros = jnp.zeros((32, 512), F32)
    dk_t = sum(dones[c][1] for c in range(n))
    dv_t = sum(dones[c][2] for c in range(n))
    result = jnp.transpose(jnp.concatenate([zeros, dk_t, dv_t, zeros], axis=0))
    out_ref[...] = result.reshape(32, 16, 128)
    mixed = (sub >= 32) & (sub < 96)
    for c in range(n):
        starts = chunks[c][0]
        held = jnp.concatenate([out_ref[pl.ds(start, 2)].reshape(32, 128) for start in starts], axis=0)
        value = jnp.where(mixed, held, dones[c][0])
        for s, start in enumerate(starts):
            out_ref[pl.ds(start, 2)] = value[s * 32 : (s + 1) * 32].reshape(2, 16, 128)


def block_kernel(
    factor, place_ref, recv_ref, scaled_ref, gate_ref, dgated_ref, cot_ref, wq_ref, wk_ref, wv_ref, wg_ref, wo_ref,
    update_ref, dnorm_ref, keep_ref, give_ref, param_ref,
):
    lane = lanes_of((512, 128))
    scaled = scaled_ref[...]
    gate = gate_ref[...]
    cot = jnp.swapaxes(cot_ref[...], 0, 1).reshape(512, 128)
    wq, wk, wv, wg = wq_ref[...], wk_ref[...], wv_ref[...], wg_ref[...]
    got = [recv_ref[:, head].reshape(512, 128) for head in range(4)]
    att = turn(got[3], 0)
    for head in range(3):
        moved = turn(got[head], 32 * head - 96)
        att = jnp.where((lane >= 32 * head) & (lane < 32 * head + 32), moved, att)
    gated = gate * att
    d_pre = dgated_ref[...] * att * gate * (1.0 - gate)
    update = dot3(gated, wo_ref[...])
    update_ref[...] = jnp.swapaxes(update.reshape(32, 16, 128), 0, 1)
    scaled_t = split(jnp.transpose(jnp.where(lane == 127, 1.0, scaled)))
    d_normed = jnp.zeros((512, 128), F32)
    for head in range(4):
        grads = split(jnp.where(lane < 96, got[head], turn(d_pre, 96 - 32 * head)))
        weights = head_weights(wq, wk, wv, wg, head, factor)
        d_normed = d_normed + dot3(grads, weights, NT)
        param_ref[head * 128 : (head + 1) * 128, :] = dot3(scaled_t, grads)
    param_ref[512:640, :] = dot3(jnp.transpose(gated), cot)
    dnorm_ref[...] = d_normed
    core = place_ref[1]
    keep_ref[...] = param_ref[pl.ds(pl.multiple_of(core * 320, 8), 320), :]
    give_ref[...] = param_ref[pl.ds(pl.multiple_of((1 - core) * 320, 8), 320), :]


def close_kernel(
    recv_ref, dnorm_ref, scaled_ref, inv_ref, gain_ref, wb_ref, grad_ref, send_ref
):
    chunk = jnp.sum(recv_ref[:, 0:10, :], axis=0)
    rows = []
    for head in range(4):
        pieces = recv_ref[head, 10:14, :]
        for z in range(1, 8):
            pieces = pieces + recv_ref[z * 4 + head, 10:14, :]
        rows.append(jnp.concatenate([pieces[a : a + 1] for a in range(4)], axis=1))
    bias_t = jnp.concatenate(rows + [jnp.zeros((4, 512), F32)], axis=0)
    scaled = scaled_ref[...]
    wide = jnp.concatenate([bias_t, jnp.zeros((120, 512), F32)], axis=0)
    wb = jnp.concatenate([wb_ref[...], jnp.zeros((124, 128), F32)], axis=0)
    d_normed = dnorm_ref[...] + dot3(jnp.transpose(wide), wb)
    d_scaled = d_normed * gain_ref[...]
    mean_term = jnp.mean(d_scaled, axis=1, keepdims=True)
    cross_term = jnp.mean(d_scaled * scaled, axis=1, keepdims=True)
    d_input = inv_ref[...] * (d_scaled - mean_term - scaled * cross_term)
    grad_ref[...] = jnp.swapaxes(d_input.reshape(32, 16, 128), 0, 1)
    bias_w = dot3(bias_t, scaled)
    tail = jnp.concatenate([chunk, bias_w[0:4], jnp.zeros((2, 128), F32)], axis=0)
    send_ref[...] = jnp.broadcast_to(tail[None], (8, 16, 128))


def share_kernel(recv_ref, send_ref):
    total = jnp.sum(recv_ref[...], axis=0)
    send_ref[...] = jnp.broadcast_to(total[None], (32, 16, 128))


def finish_kernel(
    factor, count, place_ref, own_ref, other_ref, gain_ref, wq_ref, wk_ref, wv_ref, wg_ref, wb_ref,
    q_ref, k_ref, v_ref, g_ref, shift_ref, o_ref, b_ref, gain_out_ref, own_rows, other_rows,
):
    for at in range(32):
        own_rows[at * 10 : (at + 1) * 10, :] = own_ref[at, 0:10, :]
        other_rows[at * 10 : (at + 1) * 10, :] = other_ref[at, 0:10, :]
    bias_w = jnp.sum(own_ref[:, 10:14, :], axis=0) + jnp.sum(other_ref[:, 10:14, :], axis=0)
    low_half = place_ref[1] == 0
    own_half, other_half = own_rows[...], other_rows[...]
    hold = jnp.concatenate(
        [jnp.where(low_half, own_half, other_half), jnp.where(low_half, other_half, own_half)], axis=0
    )
    wq, wk, wv, wg = wq_ref[...], wk_ref[...], wv_ref[...], wg_ref[...]
    lane = lanes_of((128, 128))
    gain_rows = jnp.transpose(jnp.broadcast_to(gain_ref[...], (128, 128)))
    last = lax.broadcasted_iota(jnp.int32, (128, 128), 0) == 127
    scale = 1.0 / count
    blocks = []
    shift = jnp.zeros((1, 128), F32)
    for head in range(4):
        block = hold[head * 128 : (head + 1) * 128, :]
        sums = turn(block[127:128], 32 * head - 96)
        shift = jnp.where((lane[0:1] >= 32 * head) & (lane[0:1] < 32 * head + 32), sums, shift)
        block = jnp.where(last, 0.0, block)
        blocks.append(jnp.where(last, -jnp.sum(block, axis=0, keepdims=True), block))
    gain_sum = jnp.zeros((128, 128), F32)
    for head in range(4):
        gain_sum = gain_sum + blocks[head] * head_weights(wq, wk, wv, wg, head, factor)
    for ref, group, times in ((q_ref, 0, factor), (k_ref, 1, 1.0), (v_ref, 2, 1.0), (g_ref, 3, 1.0)):
        full = turn(blocks[0], -32 * group)
        for head in range(1, 4):
            full = jnp.where(lane >= 32 * head, turn(blocks[head], 32 * (head - group)), full)
        ref[...] = full * gain_rows * (times * scale)
    o_ref[...] = hold[512:640, :] * scale
    b_ref[...] = bias_w * gain_ref[...] * scale
    shift_ref[...] = shift * scale
    gain_total = jnp.sum(jnp.transpose(gain_sum), axis=0, keepdims=True)
    gain_total = gain_total + jnp.sum(bias_w * wb_ref[...], axis=0, keepdims=True)
    gain_out_ref[...] = gain_total * scale


def cost(us):
    return pl.CostEstimate(flops=int(us * 1e9), bytes_accessed=int(us * 2e6), transcendentals=0)


def call(kernel, out_shape, name, us, **extra):
    return pl.pallas_call(
        kernel,
        out_shape=out_shape,
        name=name,
        cost_estimate=cost(us),
        compiler_params=pltpu.CompilerParams(vmem_limit_bytes=VMEM_BYTES),
        **extra,
    )


def shaped(*shape):
    return jax.ShapeDtypeStruct(shape, F32)


def attend_call(place, keep, data, own, other):
    columns = pl.BlockSpec((32, 16, 128), lambda j: (0, j, 0))
    slots = pl.BlockSpec((8, 32, 512), lambda j: (0, 0, 0))
    return pl.pallas_call(
        attend_kernel,
        grid=(4,),
        in_specs=[
            pl.BlockSpec(memory_space=pltpu.SMEM),
            pl.BlockSpec((4, 512), lambda j: (0, 0)),
            columns,
            slots,
            slots,
        ],
        out_specs=[columns, slots, slots],
        out_shape=[shaped(32, 64, 128), shaped(8, 32, 512), shaped(8, 32, 512)],
        name="attend",
        cost_estimate=cost(12),
        compiler_params=pltpu.CompilerParams(vmem_limit_bytes=VMEM_BYTES),
    )(place, keep, data, own, other)


def swap(value, axes):
    return lax.all_to_all(value, axes, 0, 0, tiled=False)


def partner(value, axis, flip):
    return lax.ppermute(value, axis, [(at, at ^ flip) for at in range(lax.axis_size(axis))])


def body(
    pair_rep, cotangent, chain_ids, template, norm_gain, w_query, w_key, w_value, w_gate, gate_bias, w_out, w_bias,
):
    factor = 32 ** (-0.5)
    tokens = chain_ids.shape[0]
    gain = norm_gain.reshape(1, 128)
    square = shaped(128, 128)
    row = shaped(1, 128)

    y, core = lax.axis_index("y"), lax.axis_index("core")
    first = (y * 2 + core) * 32 + lax.axis_index("z") * 4
    place = jnp.stack([y, core, first]).astype(jnp.int32)

    piece, scaled, inverse = call(
        norm_kernel, [shaped(8, 4, 4, 128), shaped(512, 128), shaped(512, 128)], "norm_bias", 1
    )(pair_rep, gain, w_bias)
    vmem = pl.BlockSpec(memory_space=pltpu.VMEM)
    send, gate, d_gated, keep = call(
        lambda *refs: project_kernel(factor, *refs),
        [shaped(8, 4, 64, 128), shaped(512, 128), shaped(512, 128), jax.ShapeDtypeStruct((4, 512), jnp.int32)],
        "project",
        2,
        in_specs=[pl.BlockSpec(memory_space=pltpu.SMEM)] + [vmem] * 11,
    )(
        place, scaled, cotangent, gain, w_query, w_key, w_value, w_gate, gate_bias.reshape(1, 128), w_out,
        chain_ids.reshape(1, 512), template,
    )

    piece = swap(piece.reshape(32, 4, 128), ROWS)
    piece, send = lax.optimization_barrier((piece, send))
    data = swap(send.reshape(32, 64, 128), ROWS)
    own = jnp.transpose(piece.reshape(32, 32, 16), (1, 0, 2)).reshape(1, 32, 512)
    own = jnp.concatenate([own] + [partner(own, "y", flip) for flip in (4, 2, 6)], axis=0)
    own = jnp.concatenate([own, partner(own, "y", 1)], axis=0)
    other = partner(own, "core", 1)

    back, d_own, d_other = attend_call(place, keep, data, own, other)

    got = swap(back, ROWS)
    d_bias = d_own + partner(d_other, "core", 1)
    d_bias = d_bias[:4] + partner(d_bias[4:], "y", 1)
    d_bias = d_bias[0] + sum(partner(d_bias[s], "y", flip) for s, flip in ((1, 4), (2, 2), (3, 6)))
    d_bias = jnp.transpose(d_bias.reshape(32, 32, 16), (1, 0, 2)).reshape(32, 4, 128)

    update, d_normed, params, give = call(
        lambda *refs: block_kernel(factor, *refs),
        [shaped(16, 32, 128), shaped(512, 128), shaped(320, 128), shaped(320, 128)],
        "block_grads",
        2,
        in_specs=[pl.BlockSpec(memory_space=pltpu.SMEM)] + [vmem] * 10,
        scratch_shapes=[pltpu.VMEM((640, 128), F32)],
    )(place, got.reshape(8, 4, 64, 128), scaled, gate, d_gated, cotangent, w_query, w_key, w_value, w_gate, w_out)

    params = params + partner(give, "core", 1)
    small = swap(jnp.concatenate([params.reshape(32, 10, 128), d_bias], axis=1), ROWS)
    grad_pair, tail = call(close_kernel, [shaped(16, 32, 128), shaped(8, 16, 128)], "norm_back", 1)(
        small, d_normed, scaled, inverse, gain, w_bias
    )
    tail = swap(tail, "y")
    tail = call(share_kernel, shaped(32, 16, 128), "share", 0.1)(tail)
    tail = swap(tail, ROWS)
    grads = call(
        lambda *refs: finish_kernel(factor, float(tokens), *refs),
        [square, square, square, square, row, square, shaped(4, 128), row],
        "finish",
        1,
        in_specs=[pl.BlockSpec(memory_space=pltpu.SMEM)] + [vmem] * 8,
        scratch_shapes=[pltpu.VMEM((320, 128), F32)] * 2,
    )(place, tail, partner(tail, "core", 1), gain, w_query, w_key, w_value, w_gate, w_bias)
    gq, gk, gv, gg, gshift, go, gb, ggain = grads
    return update, grad_pair, gq, gk, gv, gg, gshift.reshape(128), go, gb, ggain.reshape(128)


def solution(mesh):
    fine = Mesh(mesh.devices.reshape(8, 2, 8, 4), ("y", "core", "z", "x"))
    block = P(ROWS, COLS, None)
    return jax.shard_map(
        body,
        mesh=fine,
        in_specs=(block, block) + (P(),) * 10,
        out_specs=(block, block) + (P(),) * 8,
        check_vma=False,
    )
```

```python
import jax
import jax.numpy as jnp
from jax import lax
from jax.experimental import pallas as pl
from jax.experimental.pallas import tpu as pltpu
from jax.sharding import Mesh, PartitionSpec as P

F32 = jnp.float32
BF16 = jnp.bfloat16
NEG_FILL = -1000000000.0
ROWS = ("z", "x")
COLS = ("y", "core")
VMEM_BYTES = 48 * 1024 * 1024
MOST_VMEM = 60 * 1024 * 1024
NN = (((1,), (0,)), ((), ()))
NT = (((1,), (1,)), ((), ()))


def bdot(left, right, dims=NN):
    return lax.dot_general(left, right, dims, preferred_element_type=F32)


def split(value):
    high = value.astype(BF16)
    return high, (value - high.astype(F32)).astype(BF16)


def dot3(left, right, dims=NN):
    lh, ll = left if isinstance(left, tuple) else split(left)
    rh, rl = right if isinstance(right, tuple) else split(right)
    return bdot(lh, rh, dims) + (bdot(ll, rh, dims) + bdot(lh, rl, dims))


def lanes_of(shape):
    return lax.broadcasted_iota(jnp.int32, shape, 1)


def turn(value, amount):
    amount = amount % value.shape[1]
    return value if amount == 0 else pltpu.roll(value, amount, 1)


def head_weights(wq, wk, wv, wg, head, factor):
    lane = lanes_of(wq.shape)
    at = 32 * head
    out = jnp.where(lane < 32, turn(wq, -at) * factor, turn(wk, 32 - at))
    out = jnp.where(lane < 64, out, turn(wv, 64 - at))
    return jnp.where(lane < 96, out, turn(wg, 96 - at))


def norm_kernel(x_ref, gain_ref, wb_ref, piece_ref, scaled_ref, inv_ref):
    cells = jnp.swapaxes(x_ref[...], 0, 1).reshape(512, 128)
    center = jnp.mean(cells, axis=1, keepdims=True)
    shifted = cells - center
    spread = jnp.mean(shifted * shifted, axis=1, keepdims=True)
    inverse = lax.rsqrt(spread + 1e-05)
    scaled = shifted * inverse
    scaled_ref[...] = scaled
    inv_ref[...] = jnp.broadcast_to(inverse, (512, 128))
    wb = jnp.concatenate([wb_ref[...], jnp.zeros((4, 128), F32)], axis=0)
    bias = dot3(wb, scaled * gain_ref[...], NT)
    for head in range(4):
        for part in range(4):
            row = bias[head : head + 1, part * 128 : (part + 1) * 128]
            piece_ref[:, head, part, :] = jnp.broadcast_to(row, (8, 128))


def project_kernel(
    factor, place_ref, scaled_ref, cot_ref, gain_ref, wq_ref, wk_ref, wv_ref, wg_ref, gb_ref, wo_ref,
    chain_ref, template_ref, send_ref, gate_ref, dgated_ref, keep_ref,
):
    cot = jnp.swapaxes(cot_ref[...], 0, 1).reshape(512, 128)
    normed = split(scaled_ref[...] * gain_ref[...])
    wq, wk, wv, wg = wq_ref[...], wk_ref[...], wv_ref[...], wg_ref[...]
    gate = jax.nn.sigmoid(dot3(normed, wg) + gb_ref[...])
    d_gated = dot3(cot, wo_ref[...], NT)
    gate_ref[...] = gate
    dgated_ref[...] = d_gated
    d_att = d_gated * gate
    lane = lanes_of((512, 128))
    for head in range(4):
        weights = head_weights(wq, wk, wv, wg, head, factor)
        block = jnp.where(lane < 96, dot3(normed, weights), turn(d_att, 96 - 32 * head))
        send_ref[:, head] = block.reshape(8, 64, 128)
    first = place_ref[2]
    chain = chain_ref[...]
    token = lanes_of((1, 512))
    near = lanes_of((8, 8)) == first // 64
    blocks = jnp.max(jnp.where(near, template_ref[...], 0), axis=1, keepdims=True)
    open_block = jnp.zeros((1, 512), jnp.int32)
    for block in range(8):
        open_block = jnp.where(token // 64 == block, blocks[block : block + 1], open_block)
    for column in range(4):
        own = jnp.max(jnp.where(token == first + column, chain, 0), axis=1, keepdims=True)
        keep_ref[column : column + 1, :] = jnp.where(chain == own, 1, open_block)


def picker(groups):
    shape = (256, 128)
    source, lane = lax.broadcasted_iota(jnp.int32, shape, 0), lanes_of(shape)
    wanted = jnp.full(shape, -1, jnp.int32)
    for group, pick in enumerate(groups):
        if pick is not None:
            wanted = jnp.where(lane // 32 == group, pick[0] * 128 + pick[1] * 32 + lane % 32, wanted)
    return jnp.where(source == wanted, 1.0, 0.0)


def left(group):
    return [(0, group), (1, group), (0, group), (1, group)]


def right(group):
    return [(0, group), (0, group), (1, group), (1, group)]


def fill_pickers(keys_ref, rows_ref, turns_ref):
    keys = [
        right(1),
        right(2),
        [(0, 1), (1, 1), None, None],
        [(0, 1), None, None, None],
        [None, None, (1, 2), (0, 2)],
        [None, None, None, (0, 2)],
    ]
    for at, groups in enumerate(keys):
        keys_ref[:, at * 128 : (at + 1) * 128] = picker(groups).astype(BF16)
    for at, group in enumerate((0, 3)):
        pick = picker(left(group))
        rows_ref[:, at * 128 : (at + 1) * 128] = pick.astype(BF16)
        turns_ref[at * 64 : (at + 1) * 64, :] = jnp.transpose(pick)[0:64].astype(BF16)


def halves_of(value):
    high = value.astype(BF16)
    return jnp.concatenate([high, (value - high.astype(F32)).astype(BF16)], axis=1)


def attend_kernel(
    place_ref, keep_ref, data_ref, own_ref, other_ref, out_ref, d_own_ref, d_other_ref,
    keys_ref, rows_ref, turns_ref,
):
    y, core = place_ref[0], place_ref[1]
    fill_pickers(keys_ref, rows_ref, turns_ref)
    chunk_rows = 256
    per = chunk_rows // 32
    sub = lanes_of((chunk_rows, 128))
    chunks = []
    for side, (bias_ref, db_ref) in enumerate(((own_ref, d_own_ref), (other_ref, d_other_ref))):
        half = core if side == 0 else 1 - core
        for s0 in range(0, 8, per):
            starts = [(y ^ ((s >> 2) | (s & 2) | ((s & 1) << 2))) * 4 + half * 2 for s in range(s0, s0 + per)]
            chunks.append((starts, bias_ref, db_ref, s0))

    def column_keys(column):
        here = pl.ds(column * 16, 16)
        picked = bdot(halves_of(data_ref[:, here].reshape(512, 128)), keys_ref[...]).astype(BF16)
        return [picked[:, at * 128 : (at + 1) * 128] for at in range(6)] + [keep_ref[column : column + 1, :] > 0]

    def first(column, keys, chunk):
        k_right, v_right, k_both, k_first, v_both, v_first, keep = keys
        starts, bias_ref, db_ref, s0 = chunk
        here = pl.ds(column * 16, 16)
        rows = jnp.concatenate([data_ref[pl.ds(start, 2), here].reshape(32, 128) for start in starts], axis=0)
        both = halves_of(rows)
        q_left = bdot(both, rows_ref[:, 0:128]).astype(BF16)
        q_t = bdot(turns_ref[0:64], both, NT).astype(BF16)
        scores = bdot(q_left, k_right, NT) + bias_ref[s0 : s0 + per].reshape(chunk_rows, 512)
        return rows, q_t, jnp.where(keep, scores, NEG_FILL)

    def second(keys, state):
        k_right, v_right, k_both, k_first, v_both, v_first, keep = keys
        rows, q_t, scores = state
        highest = jnp.max(scores, axis=1, keepdims=True)
        weights = jnp.exp(scores - highest)
        inv_total = 1.0 / jnp.sum(weights, axis=1, keepdims=True)
        wh, wl = split(weights)
        output = bdot(wh, v_both) + bdot(wl, v_first)
        output = (output + pltpu.roll(output, 32, 1)) * inv_total
        d_out = jnp.where(sub >= 96, rows, 0.0) * inv_total
        centred = jnp.sum(d_out * output, axis=1, keepdims=True)
        d_both = halves_of(d_out)
        d_left = bdot(d_both, rows_ref[:, 128:256]).astype(BF16)
        d_weights = bdot(d_left, v_right, NT)
        d_t = bdot(turns_ref[64:128], d_both, NT).astype(BF16)
        both = bdot(d_t, wh)
        dv_t = both[0:32] + both[32:64] + bdot(d_t[0:32], wl)
        return weights, output, d_weights, centred, dv_t, q_t

    def third(column, keys, chunk, state):
        k_right, v_right, k_both, k_first, v_both, v_first, keep = keys
        starts, bias_ref, db_ref, s0 = chunk
        weights, output, d_weights, centred, dv_t, q_t = state
        d_scores = weights * (d_weights - centred)
        if column == 0:
            db_ref[s0 : s0 + per] = d_scores.reshape(per, 32, 512)
        else:
            db_ref[s0 : s0 + per] += d_scores.reshape(per, 32, 512)
        sh, sl = split(d_scores)
        d_query = bdot(sh, k_both) + bdot(sl, k_first)
        d_query = d_query + pltpu.roll(d_query, 96, 1)
        both = bdot(q_t, sh)
        dk_t = both[0:32] + both[32:64] + bdot(q_t[0:32], sl)
        return jnp.where(sub < 32, d_query, output), dk_t, dv_t

    mixed = (sub >= 32) & (sub < 96)

    def finish(column, done):
        here = pl.ds(column * 16, 16)
        zeros = jnp.zeros((32, 512), F32)
        dk_t = sum(part[1] for part in done)
        dv_t = sum(part[2] for part in done)
        result = jnp.transpose(jnp.concatenate([zeros, dk_t, dv_t, zeros], axis=0))
        out_ref[:, here] = result.reshape(32, 16, 128)
        for (starts, _, _, _), part in zip(chunks, done):
            held = jnp.concatenate([out_ref[pl.ds(start, 2), here].reshape(32, 128) for start in starts], axis=0)
            value = jnp.where(mixed, held, part[0])
            for s, start in enumerate(starts):
                out_ref[pl.ds(start, 2), here] = value[s * 32 : (s + 1) * 32].reshape(2, 16, 128)

    work = [(column, chunk) for column in range(4) for chunk in chunks]
    keys, ones, twos, dones = {}, {}, {}, {}
    for step in range(len(work) + 2):
        if step < len(work):
            column, chunk = work[step]
            if column not in keys:
                keys[column] = column_keys(column)
            ones[step] = first(column, keys[column], chunk)
        if 0 <= step - 1 < len(work):
            twos[step - 1] = second(keys[work[step - 1][0]], ones.pop(step - 1))
        if 0 <= step - 2 < len(work):
            column, chunk = work[step - 2]
            dones.setdefault(column, []).append(third(column, keys[column], chunk, twos.pop(step - 2)))
            if len(dones[column]) == len(chunks):
                finish(column, dones.pop(column))


def gate_back(got_ref, gate_ref, dgated_ref):
    lane = lanes_of((512, 128))
    gate = gate_ref[...]
    got = [got_ref[:, head].reshape(512, 128) for head in range(4)]
    att = got[3]
    for head in range(3):
        moved = turn(got[head], 32 * head - 96)
        att = jnp.where((lane >= 32 * head) & (lane < 32 * head + 32), moved, att)
    d_pre = dgated_ref[...] * att * gate * (1.0 - gate)
    grads = [jnp.where(lane < 96, got[head], turn(d_pre, 96 - 32 * head)) for head in range(4)]
    return grads, gate * att


def param_kernel(place_ref, got_ref, scaled_ref, gate_ref, dgated_ref, cot_ref, keep_ref, give_ref, param_ref):
    grads, gated = gate_back(got_ref, gate_ref, dgated_ref)
    cot = jnp.swapaxes(cot_ref[...], 0, 1).reshape(512, 128)
    scaled = jnp.where(lanes_of((512, 128)) == 127, 1.0, scaled_ref[...])
    scaled_t = split(jnp.transpose(scaled))
    for head in range(4):
        param_ref[head * 128 : (head + 1) * 128, :] = dot3(scaled_t, grads[head])
    param_ref[512:640, :] = dot3(jnp.transpose(gated), cot)
    core = place_ref[1]
    keep_ref[...] = param_ref[pl.ds(pl.multiple_of(core * 320, 8), 320), :]
    give_ref[...] = param_ref[pl.ds(pl.multiple_of((1 - core) * 320, 8), 320), :]


def update_kernel(
    factor, got_ref, gate_ref, dgated_ref, wq_ref, wk_ref, wv_ref, wg_ref, wo_ref, update_ref, dnorm_ref
):
    grads, gated = gate_back(got_ref, gate_ref, dgated_ref)
    wq, wk, wv, wg = wq_ref[...], wk_ref[...], wv_ref[...], wg_ref[...]
    update = dot3(gated, wo_ref[...])
    update_ref[...] = jnp.swapaxes(update.reshape(32, 16, 128), 0, 1)
    d_normed = jnp.zeros((512, 128), F32)
    for head in range(4):
        d_normed = d_normed + dot3(grads[head], head_weights(wq, wk, wv, wg, head, factor), NT)
    dnorm_ref[...] = d_normed


def tail_kernel(recv_ref, scaled_ref, send_ref, bias_ref):
    chunk = jnp.sum(recv_ref[:, 0:10, :], axis=0)
    rows = []
    for head in range(4):
        pieces = recv_ref[head, 10:14, :]
        for z in range(1, 8):
            pieces = pieces + recv_ref[z * 4 + head, 10:14, :]
        rows.append(jnp.concatenate([pieces[a : a + 1] for a in range(4)], axis=1))
    bias_t = jnp.concatenate(rows + [jnp.zeros((4, 512), F32)], axis=0)
    bias_ref[...] = bias_t
    bias_w = dot3(bias_t, scaled_ref[...])
    tail = jnp.concatenate([chunk, bias_w[0:4], jnp.zeros((2, 128), F32)], axis=0)
    send_ref[...] = jnp.broadcast_to(tail[None], (8, 16, 128))


def close_kernel(bias_ref, dnorm_ref, scaled_ref, inv_ref, gain_ref, wb_ref, grad_ref):
    scaled = scaled_ref[...]
    wide = jnp.concatenate([bias_ref[...], jnp.zeros((120, 512), F32)], axis=0)
    wb = jnp.concatenate([wb_ref[...], jnp.zeros((124, 128), F32)], axis=0)
    d_normed = dnorm_ref[...] + dot3(jnp.transpose(wide), wb)
    d_scaled = d_normed * gain_ref[...]
    mean_term = jnp.mean(d_scaled, axis=1, keepdims=True)
    cross_term = jnp.mean(d_scaled * scaled, axis=1, keepdims=True)
    d_input = inv_ref[...] * (d_scaled - mean_term - scaled * cross_term)
    grad_ref[...] = jnp.swapaxes(d_input.reshape(32, 16, 128), 0, 1)


def share_kernel(recv_ref, send_ref):
    total = jnp.sum(recv_ref[...], axis=0)
    send_ref[...] = jnp.broadcast_to(total[None], (32, 16, 128))


def finish_kernel(
    factor, count, place_ref, own_ref, other_ref, gain_ref, wq_ref, wk_ref, wv_ref, wg_ref, wb_ref,
    q_ref, k_ref, v_ref, g_ref, shift_ref, o_ref, b_ref, gain_out_ref, own_rows, other_rows,
):
    for at in range(32):
        own_rows[at * 10 : (at + 1) * 10, :] = own_ref[at, 0:10, :]
        other_rows[at * 10 : (at + 1) * 10, :] = other_ref[at, 0:10, :]
    bias_w = jnp.sum(own_ref[:, 10:14, :], axis=0) + jnp.sum(other_ref[:, 10:14, :], axis=0)
    low_half = place_ref[1] == 0
    own_half, other_half = own_rows[...], other_rows[...]
    hold = jnp.concatenate(
        [jnp.where(low_half, own_half, other_half), jnp.where(low_half, other_half, own_half)], axis=0
    )
    wq, wk, wv, wg = wq_ref[...], wk_ref[...], wv_ref[...], wg_ref[...]
    lane = lanes_of((128, 128))
    gain_rows = jnp.transpose(jnp.broadcast_to(gain_ref[...], (128, 128)))
    last = lax.broadcasted_iota(jnp.int32, (128, 128), 0) == 127
    scale = 1.0 / count
    blocks = []
    shift = jnp.zeros((1, 128), F32)
    for head in range(4):
        block = hold[head * 128 : (head + 1) * 128, :]
        sums = turn(block[127:128], 32 * head - 96)
        shift = jnp.where((lane[0:1] >= 32 * head) & (lane[0:1] < 32 * head + 32), sums, shift)
        block = jnp.where(last, 0.0, block)
        blocks.append(jnp.where(last, -jnp.sum(block, axis=0, keepdims=True), block))
    gain_sum = jnp.zeros((128, 128), F32)
    for head in range(4):
        gain_sum = gain_sum + blocks[head] * head_weights(wq, wk, wv, wg, head, factor)
    for ref, group, times in ((q_ref, 0, factor), (k_ref, 1, 1.0), (v_ref, 2, 1.0), (g_ref, 3, 1.0)):
        full = turn(blocks[0], -32 * group)
        for head in range(1, 4):
            full = jnp.where(lane >= 32 * head, turn(blocks[head], 32 * (head - group)), full)
        ref[...] = full * gain_rows * (times * scale)
    o_ref[...] = hold[512:640, :] * scale
    b_ref[...] = bias_w * gain_ref[...] * scale
    shift_ref[...] = shift * scale
    gain_total = jnp.sum(jnp.transpose(gain_sum), axis=0, keepdims=True)
    gain_total = gain_total + jnp.sum(bias_w * wb_ref[...], axis=0, keepdims=True)
    gain_out_ref[...] = gain_total * scale


def cost(us):
    return pl.CostEstimate(flops=int(us * 1e9), bytes_accessed=int(us * 2e6), transcendentals=0)


def call(kernel, out_shape, name, us, vmem=VMEM_BYTES, **extra):
    return pl.pallas_call(
        kernel,
        out_shape=out_shape,
        name=name,
        cost_estimate=cost(us),
        compiler_params=pltpu.CompilerParams(vmem_limit_bytes=vmem),
        **extra,
    )


def shaped(*shape):
    return jax.ShapeDtypeStruct(shape, F32)


def attend_call(place, keep, data, own, other):
    smem, vmem = pl.BlockSpec(memory_space=pltpu.SMEM), pl.BlockSpec(memory_space=pltpu.VMEM)
    return call(
        attend_kernel,
        [shaped(32, 64, 128), shaped(8, 32, 512), shaped(8, 32, 512)],
        "attend",
        12,
        in_specs=[smem] + [vmem] * 4,
        scratch_shapes=[pltpu.VMEM(shape, BF16) for shape in ((256, 768), (256, 256), (128, 256))],
    )(place, keep, data, own, other)


def swap(value, axes):
    return lax.all_to_all(value, axes, 0, 0, tiled=False)


def partner(value, axis, flip):
    return lax.ppermute(value, axis, [(at, at ^ flip) for at in range(lax.axis_size(axis))])


def body(
    pair_rep, cotangent, chain_ids, template, norm_gain, w_query, w_key, w_value, w_gate, gate_bias, w_out, w_bias,
):
    factor = 32 ** (-0.5)
    tokens = chain_ids.shape[0]
    gain = norm_gain.reshape(1, 128)
    square = shaped(128, 128)
    row = shaped(1, 128)

    y, core = lax.axis_index("y"), lax.axis_index("core")
    first = (y * 2 + core) * 32 + lax.axis_index("z") * 4
    place = jnp.stack([y, core, first]).astype(jnp.int32)

    piece, scaled, inverse = call(
        norm_kernel, [shaped(8, 4, 4, 128), shaped(512, 128), shaped(512, 128)], "norm_bias", 1, MOST_VMEM
    )(pair_rep, gain, w_bias)
    vmem = pl.BlockSpec(memory_space=pltpu.VMEM)
    send, gate, d_gated, keep = call(
        lambda *refs: project_kernel(factor, *refs),
        [shaped(8, 4, 64, 128), shaped(512, 128), shaped(512, 128), jax.ShapeDtypeStruct((4, 512), jnp.int32)],
        "project",
        2,
        MOST_VMEM,
        in_specs=[pl.BlockSpec(memory_space=pltpu.SMEM)] + [vmem] * 11,
    )(
        place, scaled, cotangent, gain, w_query, w_key, w_value, w_gate, gate_bias.reshape(1, 128), w_out,
        chain_ids.reshape(1, 512), template,
    )

    piece = swap(piece.reshape(32, 4, 128), ROWS)
    piece, send = lax.optimization_barrier((piece, send))
    data = swap(send.reshape(32, 64, 128), ROWS)
    own = jnp.transpose(piece.reshape(32, 32, 16), (1, 0, 2)).reshape(1, 32, 512)
    own = jnp.concatenate([own] + [partner(own, "y", flip) for flip in (4, 2, 6)], axis=0)
    own = jnp.concatenate([own, partner(own, "y", 1)], axis=0)
    other = partner(own, "core", 1)

    back, d_own, d_other = attend_call(place, keep, data, own, other)

    got = swap(back, ROWS)
    d_bias = d_own + partner(d_other, "core", 1)
    d_bias = d_bias[:4] + partner(d_bias[4:], "y", 1)
    d_bias = d_bias[0] + sum(partner(d_bias[s], "y", flip) for s, flip in ((1, 4), (2, 2), (3, 6)))
    d_bias = jnp.transpose(d_bias.reshape(32, 32, 16), (1, 0, 2)).reshape(32, 4, 128)

    got = got.reshape(8, 4, 64, 128)
    params, give = call(
        param_kernel,
        [shaped(320, 128), shaped(320, 128)],
        "param_grads",
        2,
        in_specs=[pl.BlockSpec(memory_space=pltpu.SMEM)] + [vmem] * 5,
        scratch_shapes=[pltpu.VMEM((640, 128), F32)],
    )(place, got, scaled, gate, d_gated, cotangent)
    update, d_normed = call(
        lambda *refs: update_kernel(factor, *refs), [shaped(16, 32, 128), shaped(512, 128)], "update", 1.5
    )(got, gate, d_gated, w_query, w_key, w_value, w_gate, w_out)

    params = params + partner(give, "core", 1)
    small = swap(jnp.concatenate([params.reshape(32, 10, 128), d_bias], axis=1), ROWS)
    tail, bias_t = call(tail_kernel, [shaped(8, 16, 128), shaped(8, 512)], "tail", 0.5)(small, scaled)
    grad_pair = call(close_kernel, shaped(16, 32, 128), "norm_back", 1)(
        bias_t, d_normed, scaled, inverse, gain, w_bias
    )
    tail = swap(tail, "y")
    tail, update, grad_pair = lax.optimization_barrier((tail, update, grad_pair))
    tail = call(share_kernel, shaped(32, 16, 128), "share", 0.1)(tail)
    tail = swap(tail, ROWS)
    grads = call(
        lambda *refs: finish_kernel(factor, float(tokens), *refs),
        [square, square, square, square, row, square, shaped(4, 128), row],
        "finish",
        1,
        in_specs=[pl.BlockSpec(memory_space=pltpu.SMEM)] + [vmem] * 8,
        scratch_shapes=[pltpu.VMEM((320, 128), F32)] * 2,
    )(place, tail, partner(tail, "core", 1), gain, w_query, w_key, w_value, w_gate, w_bias)
    gq, gk, gv, gg, gshift, go, gb, ggain = grads
    return update, grad_pair, gq, gk, gv, gg, gshift.reshape(128), go, gb, ggain.reshape(128)


def solution(mesh):
    fine = Mesh(mesh.devices.reshape(8, 2, 8, 4), ("y", "core", "z", "x"))
    block = P(ROWS, COLS, None)
    return jax.shard_map(
        body,
        mesh=fine,
        in_specs=(block, block) + (P(),) * 10,
        out_specs=(block, block) + (P(),) * 8,
        check_vma=False,
    )
```

```python
import jax
import jax.numpy as jnp
from jax import lax
from jax.experimental import pallas as pl
from jax.experimental.pallas import tpu as pltpu
from jax.sharding import Mesh, PartitionSpec as P

F32 = jnp.float32
BF16 = jnp.bfloat16
NEG_FILL = -1000000000.0
ROWS = ("z", "x")
COLS = ("y", "core")
VMEM_BYTES = 48 * 1024 * 1024
MOST_VMEM = 60 * 1024 * 1024
NN = (((1,), (0,)), ((), ()))
NT = (((1,), (1,)), ((), ()))


def bdot(left, right, dims=NN):
    return lax.dot_general(left, right, dims, preferred_element_type=F32)


def split(value):
    high = value.astype(BF16)
    return high, (value - high.astype(F32)).astype(BF16)


def dot3(left, right, dims=NN):
    lh, ll = left if isinstance(left, tuple) else split(left)
    rh, rl = right if isinstance(right, tuple) else split(right)
    return bdot(lh, rh, dims) + (bdot(ll, rh, dims) + bdot(lh, rl, dims))


def lanes_of(shape):
    return lax.broadcasted_iota(jnp.int32, shape, 1)


def turn(value, amount):
    amount = amount % value.shape[1]
    return value if amount == 0 else pltpu.roll(value, amount, 1)


def head_weights(wq, wk, wv, wg, head, factor):
    lane = lanes_of(wq.shape)
    at = 32 * head
    out = jnp.where(lane < 32, turn(wq, -at) * factor, turn(wk, 32 - at))
    out = jnp.where(lane < 64, out, turn(wv, 64 - at))
    return jnp.where(lane < 96, out, turn(wg, 96 - at))


def norm_kernel(x_ref, gain_ref, wb_ref, piece_ref, scaled_ref, inv_ref):
    cells = jnp.swapaxes(x_ref[...], 0, 1).reshape(512, 128)
    center = jnp.mean(cells, axis=1, keepdims=True)
    shifted = cells - center
    spread = jnp.mean(shifted * shifted, axis=1, keepdims=True)
    inverse = lax.rsqrt(spread + 1e-05)
    scaled = shifted * inverse
    scaled_ref[...] = scaled
    inv_ref[...] = jnp.broadcast_to(inverse, (512, 128))
    wb = jnp.concatenate([wb_ref[...], jnp.zeros((4, 128), F32)], axis=0)
    bias = dot3(wb, scaled * gain_ref[...], NT)
    for head in range(4):
        for part in range(4):
            row = bias[head : head + 1, part * 128 : (part + 1) * 128]
            piece_ref[:, head, part, :] = jnp.broadcast_to(row, (8, 128))


def project_kernel(
    factor, place_ref, scaled_ref, cot_ref, gain_ref, wq_ref, wk_ref, wv_ref, wg_ref, gb_ref, wo_ref,
    chain_ref, template_ref, send_ref, gate_ref, dgated_ref, keep_ref,
):
    cot = jnp.swapaxes(cot_ref[...], 0, 1).reshape(512, 128)
    normed = split(scaled_ref[...] * gain_ref[...])
    wq, wk, wv, wg = wq_ref[...], wk_ref[...], wv_ref[...], wg_ref[...]
    gate = jax.nn.sigmoid(dot3(normed, wg) + gb_ref[...])
    d_gated = dot3(cot, wo_ref[...], NT)
    gate_ref[...] = gate
    dgated_ref[...] = d_gated
    d_att = d_gated * gate
    lane = lanes_of((512, 128))
    for head in range(4):
        weights = head_weights(wq, wk, wv, wg, head, factor)
        block = jnp.where(lane < 96, dot3(normed, weights), turn(d_att, 96 - 32 * head))
        send_ref[:, head] = block.reshape(8, 64, 128)
    first = place_ref[2]
    chain = chain_ref[...]
    token = lanes_of((1, 512))
    near = lanes_of((8, 8)) == first // 64
    blocks = jnp.max(jnp.where(near, template_ref[...], 0), axis=1, keepdims=True)
    open_block = jnp.zeros((1, 512), jnp.int32)
    for block in range(8):
        open_block = jnp.where(token // 64 == block, blocks[block : block + 1], open_block)
    for column in range(4):
        own = jnp.max(jnp.where(token == first + column, chain, 0), axis=1, keepdims=True)
        keep_ref[column : column + 1, :] = jnp.where(chain == own, 1, open_block)


def picker(groups):
    shape = (256, 128)
    source, lane = lax.broadcasted_iota(jnp.int32, shape, 0), lanes_of(shape)
    wanted = jnp.full(shape, -1, jnp.int32)
    for group, pick in enumerate(groups):
        if pick is not None:
            wanted = jnp.where(lane // 32 == group, pick[0] * 128 + pick[1] * 32 + lane % 32, wanted)
    return jnp.where(source == wanted, 1.0, 0.0)


def left(group):
    return [(0, group), (1, group), (0, group), (1, group)]


def right(group):
    return [(0, group), (0, group), (1, group), (1, group)]


def fill_pickers(keys_ref, rows_ref, turns_ref):
    keys = [
        right(1),
        right(2),
        [(0, 1), (1, 1), None, None],
        [(0, 1), None, None, None],
        [None, None, (1, 2), (0, 2)],
        [None, None, None, (0, 2)],
    ]
    for at, groups in enumerate(keys):
        keys_ref[:, at * 128 : (at + 1) * 128] = picker(groups).astype(BF16)
    for at, group in enumerate((0, 3)):
        pick = picker(left(group))
        rows_ref[:, at * 128 : (at + 1) * 128] = pick.astype(BF16)
        turns_ref[at * 64 : (at + 1) * 64, :] = jnp.transpose(pick)[0:64].astype(BF16)


def halves_of(value):
    high = value.astype(BF16)
    return jnp.concatenate([high, (value - high.astype(F32)).astype(BF16)], axis=1)


def attend_kernel(
    place_ref, keep_ref, data_ref, own_low_ref, own_high_ref, other_low_ref, other_high_ref,
    out_ref, d_own_ref, d_other_ref,
    keys_ref, rows_ref, turns_ref,
):
    y, core = place_ref[0], place_ref[1]
    fill_pickers(keys_ref, rows_ref, turns_ref)
    chunk_rows = 256
    per = chunk_rows // 32
    sub = lanes_of((chunk_rows, 128))
    chunks = []
    sides = (((own_low_ref, own_high_ref), d_own_ref), ((other_low_ref, other_high_ref), d_other_ref))
    for side, (bias_refs, db_ref) in enumerate(sides):
        half = core if side == 0 else 1 - core
        for s0 in range(0, 8, per):
            starts = [(y ^ ((s >> 2) | (s & 2) | ((s & 1) << 2))) * 4 + half * 2 for s in range(s0, s0 + per)]
            chunks.append((starts, bias_refs, db_ref, s0))

    def column_keys(column):
        here = pl.ds(column * 16, 16)
        picked = bdot(halves_of(data_ref[:, here].reshape(512, 128)), keys_ref[...]).astype(BF16)
        return [picked[:, at * 128 : (at + 1) * 128] for at in range(6)] + [keep_ref[column : column + 1, :] > 0]

    def first(column, keys, chunk):
        k_right, v_right, k_both, k_first, v_both, v_first, keep = keys
        starts, bias_refs, db_ref, s0 = chunk
        here = pl.ds(column * 16, 16)
        rows = jnp.concatenate([data_ref[pl.ds(start, 2), here].reshape(32, 128) for start in starts], axis=0)
        both = halves_of(rows)
        q_left = bdot(both, rows_ref[:, 0:128]).astype(BF16)
        q_t = bdot(turns_ref[0:64], both, NT).astype(BF16)
        bias = jnp.concatenate([ref[...].reshape(128, 512) for ref in bias_refs], axis=0)
        scores = bdot(q_left, k_right, NT) + bias
        return rows, q_t, jnp.where(keep, scores, NEG_FILL)

    def second(keys, state):
        k_right, v_right, k_both, k_first, v_both, v_first, keep = keys
        rows, q_t, scores = state
        highest = jnp.max(scores, axis=1, keepdims=True)
        weights = jnp.exp(scores - highest)
        inv_total = 1.0 / jnp.sum(weights, axis=1, keepdims=True)
        wh, wl = split(weights)
        output = bdot(wh, v_both) + bdot(wl, v_first)
        output = (output + pltpu.roll(output, 32, 1)) * inv_total
        d_out = jnp.where(sub >= 96, rows, 0.0) * inv_total
        centred = jnp.sum(d_out * output, axis=1, keepdims=True)
        d_both = halves_of(d_out)
        d_left = bdot(d_both, rows_ref[:, 128:256]).astype(BF16)
        d_weights = bdot(d_left, v_right, NT)
        d_t = bdot(turns_ref[64:128], d_both, NT).astype(BF16)
        both = bdot(d_t, wh)
        dv_t = both[0:32] + both[32:64] + bdot(d_t[0:32], wl)
        return weights, output, d_weights, centred, dv_t, q_t

    def third(column, keys, chunk, state):
        k_right, v_right, k_both, k_first, v_both, v_first, keep = keys
        starts, bias_refs, db_ref, s0 = chunk
        weights, output, d_weights, centred, dv_t, q_t = state
        d_scores = weights * (d_weights - centred)
        if column == 0:
            db_ref[s0 : s0 + per] = d_scores.reshape(per, 32, 512)
        else:
            db_ref[s0 : s0 + per] += d_scores.reshape(per, 32, 512)
        sh, sl = split(d_scores)
        d_query = bdot(sh, k_both) + bdot(sl, k_first)
        d_query = d_query + pltpu.roll(d_query, 96, 1)
        both = bdot(q_t, sh)
        dk_t = both[0:32] + both[32:64] + bdot(q_t[0:32], sl)
        return jnp.where(sub < 32, d_query, output), dk_t, dv_t

    mixed = (sub >= 32) & (sub < 96)

    def finish(column, done):
        here = pl.ds(column * 16, 16)
        zeros = jnp.zeros((32, 512), F32)
        dk_t = sum(part[1] for part in done)
        dv_t = sum(part[2] for part in done)
        result = jnp.transpose(jnp.concatenate([zeros, dk_t, dv_t, zeros], axis=0))
        out_ref[:, here] = result.reshape(32, 16, 128)
        for (starts, _, _, _), part in zip(chunks, done):
            held = jnp.concatenate([out_ref[pl.ds(start, 2), here].reshape(32, 128) for start in starts], axis=0)
            value = jnp.where(mixed, held, part[0])
            for s, start in enumerate(starts):
                out_ref[pl.ds(start, 2), here] = value[s * 32 : (s + 1) * 32].reshape(2, 16, 128)

    work = [(column, chunk) for column in range(4) for chunk in chunks]
    keys, ones, twos, dones = {}, {}, {}, {}
    for step in range(len(work) + 2):
        if step < len(work):
            column, chunk = work[step]
            if column not in keys:
                keys[column] = column_keys(column)
            ones[step] = first(column, keys[column], chunk)
        if 0 <= step - 1 < len(work):
            twos[step - 1] = second(keys[work[step - 1][0]], ones.pop(step - 1))
        if 0 <= step - 2 < len(work):
            column, chunk = work[step - 2]
            dones.setdefault(column, []).append(third(column, keys[column], chunk, twos.pop(step - 2)))
            if len(dones[column]) == len(chunks):
                finish(column, dones.pop(column))


def gate_back(got_ref, gate_ref, dgated_ref):
    lane = lanes_of((512, 128))
    gate = gate_ref[...]
    got = [got_ref[:, head].reshape(512, 128) for head in range(4)]
    att = got[3]
    for head in range(3):
        moved = turn(got[head], 32 * head - 96)
        att = jnp.where((lane >= 32 * head) & (lane < 32 * head + 32), moved, att)
    d_pre = dgated_ref[...] * att * gate * (1.0 - gate)
    grads = [jnp.where(lane < 96, got[head], turn(d_pre, 96 - 32 * head)) for head in range(4)]
    return grads, gate * att


def param_kernel(place_ref, got_ref, scaled_ref, gate_ref, dgated_ref, cot_ref, keep_ref, give_ref, param_ref):
    grads, gated = gate_back(got_ref, gate_ref, dgated_ref)
    cot = jnp.swapaxes(cot_ref[...], 0, 1).reshape(512, 128)
    scaled = jnp.where(lanes_of((512, 128)) == 127, 1.0, scaled_ref[...])
    scaled_t = split(jnp.transpose(scaled))
    for head in range(4):
        param_ref[head * 128 : (head + 1) * 128, :] = dot3(scaled_t, grads[head])
    param_ref[512:640, :] = dot3(jnp.transpose(gated), cot)
    core = place_ref[1]
    keep_ref[...] = param_ref[pl.ds(pl.multiple_of(core * 320, 8), 320), :]
    give_ref[...] = param_ref[pl.ds(pl.multiple_of((1 - core) * 320, 8), 320), :]


def update_kernel(
    factor, got_ref, gate_ref, dgated_ref, wq_ref, wk_ref, wv_ref, wg_ref, wo_ref, update_ref, dnorm_ref
):
    grads, gated = gate_back(got_ref, gate_ref, dgated_ref)
    wq, wk, wv, wg = wq_ref[...], wk_ref[...], wv_ref[...], wg_ref[...]
    update = dot3(gated, wo_ref[...])
    update_ref[...] = jnp.swapaxes(update.reshape(32, 16, 128), 0, 1)
    d_normed = jnp.zeros((512, 128), F32)
    for head in range(4):
        d_normed = d_normed + dot3(grads[head], head_weights(wq, wk, wv, wg, head, factor), NT)
    dnorm_ref[...] = d_normed


def tail_kernel(recv_ref, scaled_ref, send_ref, bias_ref):
    chunk = jnp.sum(recv_ref[:, 0:10, :], axis=0)
    rows = []
    for head in range(4):
        pieces = recv_ref[head, 10:14, :]
        for z in range(1, 8):
            pieces = pieces + recv_ref[z * 4 + head, 10:14, :]
        rows.append(jnp.concatenate([pieces[a : a + 1] for a in range(4)], axis=1))
    bias_t = jnp.concatenate(rows + [jnp.zeros((4, 512), F32)], axis=0)
    bias_ref[...] = bias_t
    bias_w = dot3(bias_t, scaled_ref[...])
    tail = jnp.concatenate([chunk, bias_w[0:4], jnp.zeros((2, 128), F32)], axis=0)
    send_ref[...] = jnp.broadcast_to(tail[None], (8, 16, 128))


def close_kernel(bias_ref, dnorm_ref, scaled_ref, inv_ref, gain_ref, wb_ref, grad_ref):
    scaled = scaled_ref[...]
    wide = jnp.concatenate([bias_ref[...], jnp.zeros((120, 512), F32)], axis=0)
    wb = jnp.concatenate([wb_ref[...], jnp.zeros((124, 128), F32)], axis=0)
    d_normed = dnorm_ref[...] + dot3(jnp.transpose(wide), wb)
    d_scaled = d_normed * gain_ref[...]
    mean_term = jnp.mean(d_scaled, axis=1, keepdims=True)
    cross_term = jnp.mean(d_scaled * scaled, axis=1, keepdims=True)
    d_input = inv_ref[...] * (d_scaled - mean_term - scaled * cross_term)
    grad_ref[...] = jnp.swapaxes(d_input.reshape(32, 16, 128), 0, 1)


def share_kernel(recv_ref, send_ref):
    total = jnp.sum(recv_ref[...], axis=0)
    send_ref[...] = jnp.broadcast_to(total[None], (32, 16, 128))


def finish_kernel(
    factor, count, place_ref, own_ref, other_ref, gain_ref, wq_ref, wk_ref, wv_ref, wg_ref, wb_ref,
    q_ref, k_ref, v_ref, g_ref, shift_ref, o_ref, b_ref, gain_out_ref, own_rows, other_rows,
):
    for at in range(32):
        own_rows[at * 10 : (at + 1) * 10, :] = own_ref[at, 0:10, :]
        other_rows[at * 10 : (at + 1) * 10, :] = other_ref[at, 0:10, :]
    bias_w = jnp.sum(own_ref[:, 10:14, :], axis=0) + jnp.sum(other_ref[:, 10:14, :], axis=0)
    low_half = place_ref[1] == 0
    own_half, other_half = own_rows[...], other_rows[...]
    hold = jnp.concatenate(
        [jnp.where(low_half, own_half, other_half), jnp.where(low_half, other_half, own_half)], axis=0
    )
    wq, wk, wv, wg = wq_ref[...], wk_ref[...], wv_ref[...], wg_ref[...]
    lane = lanes_of((128, 128))
    gain_rows = jnp.transpose(jnp.broadcast_to(gain_ref[...], (128, 128)))
    last = lax.broadcasted_iota(jnp.int32, (128, 128), 0) == 127
    scale = 1.0 / count
    blocks = []
    shift = jnp.zeros((1, 128), F32)
    for head in range(4):
        block = hold[head * 128 : (head + 1) * 128, :]
        sums = turn(block[127:128], 32 * head - 96)
        shift = jnp.where((lane[0:1] >= 32 * head) & (lane[0:1] < 32 * head + 32), sums, shift)
        block = jnp.where(last, 0.0, block)
        blocks.append(jnp.where(last, -jnp.sum(block, axis=0, keepdims=True), block))
    gain_sum = jnp.zeros((128, 128), F32)
    for head in range(4):
        gain_sum = gain_sum + blocks[head] * head_weights(wq, wk, wv, wg, head, factor)
    for ref, group, times in ((q_ref, 0, factor), (k_ref, 1, 1.0), (v_ref, 2, 1.0), (g_ref, 3, 1.0)):
        full = turn(blocks[0], -32 * group)
        for head in range(1, 4):
            full = jnp.where(lane >= 32 * head, turn(blocks[head], 32 * (head - group)), full)
        ref[...] = full * gain_rows * (times * scale)
    o_ref[...] = hold[512:640, :] * scale
    b_ref[...] = bias_w * gain_ref[...] * scale
    shift_ref[...] = shift * scale
    gain_total = jnp.sum(jnp.transpose(gain_sum), axis=0, keepdims=True)
    gain_total = gain_total + jnp.sum(bias_w * wb_ref[...], axis=0, keepdims=True)
    gain_out_ref[...] = gain_total * scale


def cost(us):
    return pl.CostEstimate(flops=int(us * 1e9), bytes_accessed=int(us * 2e6), transcendentals=0)


def call(kernel, out_shape, name, us, vmem=VMEM_BYTES, **extra):
    return pl.pallas_call(
        kernel,
        out_shape=out_shape,
        name=name,
        cost_estimate=cost(us),
        compiler_params=pltpu.CompilerParams(vmem_limit_bytes=vmem),
        **extra,
    )


def shaped(*shape):
    return jax.ShapeDtypeStruct(shape, F32)


def attend_call(place, keep, data, *bias):
    smem, vmem = pl.BlockSpec(memory_space=pltpu.SMEM), pl.BlockSpec(memory_space=pltpu.VMEM)
    return call(
        attend_kernel,
        [shaped(32, 64, 128), shaped(8, 32, 512), shaped(8, 32, 512)],
        "attend",
        12,
        in_specs=[smem] + [vmem] * 6,
        scratch_shapes=[pltpu.VMEM(shape, BF16) for shape in ((256, 768), (256, 256), (128, 256))],
    )(place, keep, data, *bias)


def swap(value, axes):
    return lax.all_to_all(value, axes, 0, 0, tiled=False)


def partner(value, axis, flip):
    return lax.ppermute(value, axis, [(at, at ^ flip) for at in range(lax.axis_size(axis))])


def body(
    pair_rep, cotangent, chain_ids, template, norm_gain, w_query, w_key, w_value, w_gate, gate_bias, w_out, w_bias,
):
    factor = 32 ** (-0.5)
    tokens = chain_ids.shape[0]
    gain = norm_gain.reshape(1, 128)
    square = shaped(128, 128)
    row = shaped(1, 128)

    y, core = lax.axis_index("y"), lax.axis_index("core")
    first = (y * 2 + core) * 32 + lax.axis_index("z") * 4
    place = jnp.stack([y, core, first]).astype(jnp.int32)

    piece, scaled, inverse = call(
        norm_kernel, [shaped(8, 4, 4, 128), shaped(512, 128), shaped(512, 128)], "norm_bias", 1, MOST_VMEM
    )(pair_rep, gain, w_bias)
    vmem = pl.BlockSpec(memory_space=pltpu.VMEM)
    send, gate, d_gated, keep = call(
        lambda *refs: project_kernel(factor, *refs),
        [shaped(8, 4, 64, 128), shaped(512, 128), shaped(512, 128), jax.ShapeDtypeStruct((4, 512), jnp.int32)],
        "project",
        2,
        MOST_VMEM,
        in_specs=[pl.BlockSpec(memory_space=pltpu.SMEM)] + [vmem] * 11,
    )(
        place, scaled, cotangent, gain, w_query, w_key, w_value, w_gate, gate_bias.reshape(1, 128), w_out,
        chain_ids.reshape(1, 512), template,
    )

    piece = swap(piece.reshape(32, 4, 128), ROWS)
    piece, send = lax.optimization_barrier((piece, send))
    data = swap(send.reshape(32, 64, 128), ROWS)
    own = jnp.transpose(piece.reshape(32, 32, 16), (1, 0, 2)).reshape(1, 32, 512)
    near = jnp.concatenate([own, partner(own, "y", 4)], axis=0)
    far = jnp.concatenate([partner(own, "y", 2), partner(own, "y", 6)], axis=0)
    low = jnp.concatenate([near, far], axis=0)
    high = jnp.concatenate([partner(near, "y", 1), partner(far, "y", 1)], axis=0)
    bias = [low, high, partner(low, "core", 1), partner(high, "core", 1)]

    back, d_own, d_other = attend_call(place, keep, data, *bias)

    got = swap(back, ROWS)
    d_bias = d_own + partner(d_other, "core", 1)
    d_bias = d_bias[:4] + partner(d_bias[4:], "y", 1)
    d_bias = d_bias[0] + sum(partner(d_bias[s], "y", flip) for s, flip in ((1, 4), (2, 2), (3, 6)))
    d_bias = jnp.transpose(d_bias.reshape(32, 32, 16), (1, 0, 2)).reshape(32, 4, 128)

    got = got.reshape(8, 4, 64, 128)
    params, give = call(
        param_kernel,
        [shaped(320, 128), shaped(320, 128)],
        "param_grads",
        2,
        in_specs=[pl.BlockSpec(memory_space=pltpu.SMEM)] + [vmem] * 5,
        scratch_shapes=[pltpu.VMEM((640, 128), F32)],
    )(place, got, scaled, gate, d_gated, cotangent)
    update, d_normed = call(
        lambda *refs: update_kernel(factor, *refs), [shaped(16, 32, 128), shaped(512, 128)], "update", 1.5
    )(got, gate, d_gated, w_query, w_key, w_value, w_gate, w_out)

    params = params + partner(give, "core", 1)
    small = swap(jnp.concatenate([params.reshape(32, 10, 128), d_bias], axis=1), ROWS)
    tail, bias_t = call(tail_kernel, [shaped(8, 16, 128), shaped(8, 512)], "tail", 0.5)(small, scaled)
    grad_pair = call(close_kernel, shaped(16, 32, 128), "norm_back", 1)(
        bias_t, d_normed, scaled, inverse, gain, w_bias
    )
    tail = swap(tail, "y")
    tail, update, grad_pair = lax.optimization_barrier((tail, update, grad_pair))
    tail = call(share_kernel, shaped(32, 16, 128), "share", 0.1)(tail)
    tail = swap(tail, ROWS)
    grads = call(
        lambda *refs: finish_kernel(factor, float(tokens), *refs),
        [square, square, square, square, row, square, shaped(4, 128), row],
        "finish",
        1,
        in_specs=[pl.BlockSpec(memory_space=pltpu.SMEM)] + [vmem] * 8,
        scratch_shapes=[pltpu.VMEM((320, 128), F32)] * 2,
    )(place, tail, partner(tail, "core", 1), gain, w_query, w_key, w_value, w_gate, w_bias)
    gq, gk, gv, gg, gshift, go, gb, ggain = grads
    return update, grad_pair, gq, gk, gv, gg, gshift.reshape(128), go, gb, ggain.reshape(128)


def solution(mesh):
    fine = Mesh(mesh.devices.reshape(8, 2, 8, 4), ("y", "core", "z", "x"))
    block = P(ROWS, COLS, None)
    return jax.shard_map(
        body,
        mesh=fine,
        in_specs=(block, block) + (P(),) * 10,
        out_specs=(block, block) + (P(),) * 8,
        check_vma=False,
    )
```

```python
import jax
import jax.numpy as jnp
from jax import lax
from jax.experimental import pallas as pl
from jax.experimental.pallas import tpu as pltpu
from jax.sharding import Mesh, PartitionSpec as P

F32 = jnp.float32
BF16 = jnp.bfloat16
NEG_FILL = -1000000000.0
ROWS = ("z", "x")
COLS = ("y", "core")
VMEM_BYTES = 48 * 1024 * 1024
MOST_VMEM = 60 * 1024 * 1024
NN = (((1,), (0,)), ((), ()))
NT = (((1,), (1,)), ((), ()))


def bdot(left, right, dims=NN):
    return lax.dot_general(left, right, dims, preferred_element_type=F32)


def split(value):
    high = value.astype(BF16)
    return high, (value - high.astype(F32)).astype(BF16)


def dot3(left, right, dims=NN):
    lh, ll = left if isinstance(left, tuple) else split(left)
    rh, rl = right if isinstance(right, tuple) else split(right)
    return bdot(lh, rh, dims) + (bdot(ll, rh, dims) + bdot(lh, rl, dims))


def lanes_of(shape):
    return lax.broadcasted_iota(jnp.int32, shape, 1)


def turn(value, amount):
    amount = amount % value.shape[1]
    return value if amount == 0 else pltpu.roll(value, amount, 1)


def head_weights(wq, wk, wv, wg, head, factor):
    lane = lanes_of(wq.shape)
    at = 32 * head
    out = jnp.where(lane < 32, turn(wq, -at) * factor, turn(wk, 32 - at))
    out = jnp.where(lane < 64, out, turn(wv, 64 - at))
    return jnp.where(lane < 96, out, turn(wg, 96 - at))


def norm_kernel(x_ref, gain_ref, wb_ref, piece_ref, scaled_ref, inv_ref):
    cells = jnp.swapaxes(x_ref[...], 0, 1).reshape(512, 128)
    center = jnp.mean(cells, axis=1, keepdims=True)
    shifted = cells - center
    spread = jnp.mean(shifted * shifted, axis=1, keepdims=True)
    inverse = lax.rsqrt(spread + 1e-05)
    scaled = shifted * inverse
    scaled_ref[...] = scaled
    inv_ref[...] = jnp.broadcast_to(inverse, (512, 128))
    wb = jnp.concatenate([wb_ref[...], jnp.zeros((4, 128), F32)], axis=0)
    bias = dot3(wb, scaled * gain_ref[...], NT)
    for head in range(4):
        for part in range(4):
            row = bias[head : head + 1, part * 128 : (part + 1) * 128]
            piece_ref[:, head, part, :] = jnp.broadcast_to(row, (8, 128))


def project_kernel(
    factor, place_ref, scaled_ref, cot_ref, gain_ref, wq_ref, wk_ref, wv_ref, wg_ref, gb_ref, wo_ref,
    chain_ref, template_ref, send_ref, gate_ref, dgated_ref, keep_ref,
):
    cot = jnp.swapaxes(cot_ref[...], 0, 1).reshape(512, 128)
    normed = split(scaled_ref[...] * gain_ref[...])
    wq, wk, wv, wg = wq_ref[...], wk_ref[...], wv_ref[...], wg_ref[...]
    gate = jax.nn.sigmoid(dot3(normed, wg) + gb_ref[...])
    d_gated = dot3(cot, wo_ref[...], NT)
    gate_ref[...] = gate
    dgated_ref[...] = d_gated
    d_att = d_gated * gate
    lane = lanes_of((512, 128))
    for head in range(4):
        weights = head_weights(wq, wk, wv, wg, head, factor)
        block = jnp.where(lane < 96, dot3(normed, weights), turn(d_att, 96 - 32 * head))
        send_ref[:, head] = block.reshape(8, 64, 128)
    first = place_ref[2]
    chain = chain_ref[...]
    token = lanes_of((1, 512))
    near = lanes_of((8, 8)) == first // 64
    blocks = jnp.max(jnp.where(near, template_ref[...], 0), axis=1, keepdims=True)
    open_block = jnp.zeros((1, 512), jnp.int32)
    for block in range(8):
        open_block = jnp.where(token // 64 == block, blocks[block : block + 1], open_block)
    for column in range(4):
        own = jnp.max(jnp.where(token == first + column, chain, 0), axis=1, keepdims=True)
        keep_ref[column : column + 1, :] = jnp.where(chain == own, 1, open_block)


def picker(groups):
    shape = (256, 128)
    source, lane = lax.broadcasted_iota(jnp.int32, shape, 0), lanes_of(shape)
    wanted = jnp.full(shape, -1, jnp.int32)
    for group, pick in enumerate(groups):
        if pick is not None:
            wanted = jnp.where(lane // 32 == group, pick[0] * 128 + pick[1] * 32 + lane % 32, wanted)
    return jnp.where(source == wanted, 1.0, 0.0)


def left(group):
    return [(0, group), (1, group), (0, group), (1, group)]


def right(group):
    return [(0, group), (0, group), (1, group), (1, group)]


def fill_pickers(keys_ref, rows_ref, turns_ref):
    keys = [
        right(1),
        right(2),
        [(0, 1), (1, 1), None, None],
        [(0, 1), None, None, None],
        [None, None, (1, 2), (0, 2)],
        [None, None, None, (0, 2)],
    ]
    for at, groups in enumerate(keys):
        keys_ref[:, at * 128 : (at + 1) * 128] = picker(groups).astype(BF16)
    for at, group in enumerate((0, 3)):
        pick = picker(left(group))
        rows_ref[:, at * 128 : (at + 1) * 128] = pick.astype(BF16)
        turns_ref[at * 64 : (at + 1) * 64, :] = jnp.transpose(pick)[0:64].astype(BF16)


def halves_of(value):
    high = value.astype(BF16)
    return jnp.concatenate([high, (value - high.astype(F32)).astype(BF16)], axis=1)


def attend_kernel(
    place_ref, keep_ref, data_ref, own_low_ref, own_high_ref, other_low_ref, other_high_ref,
    out_ref, d_own_ref, d_other_ref,
    keys_ref, rows_ref, turns_ref,
):
    y, core = place_ref[0], place_ref[1]
    fill_pickers(keys_ref, rows_ref, turns_ref)
    chunk_rows = 256
    per = chunk_rows // 32
    sub = lanes_of((chunk_rows, 128))
    chunks = []
    sides = (((own_low_ref, own_high_ref), d_own_ref), ((other_low_ref, other_high_ref), d_other_ref))
    for side, (bias_refs, db_ref) in enumerate(sides):
        half = core if side == 0 else 1 - core
        for s0 in range(0, 8, per):
            starts = [(y ^ ((s >> 2) | (s & 2) | ((s & 1) << 2))) * 4 + half * 2 for s in range(s0, s0 + per)]
            chunks.append((starts, bias_refs, db_ref, s0))

    def column_keys(column):
        here = pl.ds(column * 16, 16)
        picked = bdot(halves_of(data_ref[:, here].reshape(512, 128)), keys_ref[...]).astype(BF16)
        return [picked[:, at * 128 : (at + 1) * 128] for at in range(6)] + [keep_ref[column : column + 1, :] > 0]

    def first(column, keys, chunk):
        k_right, v_right, k_both, k_first, v_both, v_first, keep = keys
        starts, bias_refs, db_ref, s0 = chunk
        here = pl.ds(column * 16, 16)
        rows = jnp.concatenate([data_ref[pl.ds(start, 2), here].reshape(32, 128) for start in starts], axis=0)
        both = halves_of(rows)
        q_left = bdot(both, rows_ref[:, 0:128]).astype(BF16)
        q_t = bdot(turns_ref[0:64], both, NT).astype(BF16)
        bias = jnp.concatenate([ref[...].reshape(128, 512) for ref in bias_refs], axis=0)
        scores = bdot(q_left, k_right, NT) + bias
        return rows, q_t, jnp.where(keep, scores, NEG_FILL)

    def second(keys, state):
        k_right, v_right, k_both, k_first, v_both, v_first, keep = keys
        rows, q_t, scores = state
        highest = jnp.max(scores, axis=1, keepdims=True)
        weights = jnp.exp(scores - highest)
        inv_total = 1.0 / jnp.sum(weights, axis=1, keepdims=True)
        wh, wl = split(weights)
        output = bdot(wh, v_both) + bdot(wl, v_first)
        output = (output + pltpu.roll(output, 32, 1)) * inv_total
        d_out = jnp.where(sub >= 96, rows, 0.0) * inv_total
        centred = jnp.sum(d_out * output, axis=1, keepdims=True)
        d_both = halves_of(d_out)
        d_left = bdot(d_both, rows_ref[:, 128:256]).astype(BF16)
        d_weights = bdot(d_left, v_right, NT)
        d_t = bdot(turns_ref[64:128], d_both, NT).astype(BF16)
        return weights, output, d_weights, centred, (d_t, wh, wl), q_t

    def third(column, keys, chunk, state):
        k_right, v_right, k_both, k_first, v_both, v_first, keep = keys
        starts, bias_refs, db_ref, s0 = chunk
        weights, output, d_weights, centred, (d_t, wh, wl), q_t = state
        both = bdot(d_t, wh)
        dv_t = both[0:32] + both[32:64] + bdot(d_t[0:32], wl)
        d_scores = weights * (d_weights - centred)
        if column == 0:
            db_ref[s0 : s0 + per] = d_scores.reshape(per, 32, 512)
        else:
            db_ref[s0 : s0 + per] += d_scores.reshape(per, 32, 512)
        sh, sl = split(d_scores)
        d_query = bdot(sh, k_both) + bdot(sl, k_first)
        d_query = d_query + pltpu.roll(d_query, 96, 1)
        both = bdot(q_t, sh)
        dk_t = both[0:32] + both[32:64] + bdot(q_t[0:32], sl)
        return jnp.where(sub < 32, d_query, output), dk_t, dv_t

    mixed = (sub >= 32) & (sub < 96)

    def finish(column, done):
        here = pl.ds(column * 16, 16)
        zeros = jnp.zeros((32, 512), F32)
        dk_t = sum(part[1] for part in done)
        dv_t = sum(part[2] for part in done)
        result = jnp.transpose(jnp.concatenate([zeros, dk_t, dv_t, zeros], axis=0))
        out_ref[:, here] = result.reshape(32, 16, 128)
        for (starts, _, _, _), part in zip(chunks, done):
            held = jnp.concatenate([out_ref[pl.ds(start, 2), here].reshape(32, 128) for start in starts], axis=0)
            value = jnp.where(mixed, held, part[0])
            for s, start in enumerate(starts):
                out_ref[pl.ds(start, 2), here] = value[s * 32 : (s + 1) * 32].reshape(2, 16, 128)

    work = [(column, chunk) for column in range(4) for chunk in chunks]
    keys, ones, twos, dones = {}, {}, {}, {}
    for step in range(len(work) + 2):
        if step < len(work):
            column, chunk = work[step]
            if column not in keys:
                keys[column] = column_keys(column)
            ones[step] = first(column, keys[column], chunk)
        if 0 <= step - 1 < len(work):
            twos[step - 1] = second(keys[work[step - 1][0]], ones.pop(step - 1))
        if 0 <= step - 2 < len(work):
            column, chunk = work[step - 2]
            dones.setdefault(column, []).append(third(column, keys[column], chunk, twos.pop(step - 2)))
            if len(dones[column]) == len(chunks):
                finish(column, dones.pop(column))


def gate_back(got_ref, gate_ref, dgated_ref):
    lane = lanes_of((512, 128))
    gate = gate_ref[...]
    got = [got_ref[:, head].reshape(512, 128) for head in range(4)]
    att = got[3]
    for head in range(3):
        moved = turn(got[head], 32 * head - 96)
        att = jnp.where((lane >= 32 * head) & (lane < 32 * head + 32), moved, att)
    d_pre = dgated_ref[...] * att * gate * (1.0 - gate)
    grads = [jnp.where(lane < 96, got[head], turn(d_pre, 96 - 32 * head)) for head in range(4)]
    return grads, gate * att


def param_kernel(place_ref, got_ref, scaled_ref, gate_ref, dgated_ref, cot_ref, keep_ref, give_ref, param_ref):
    grads, gated = gate_back(got_ref, gate_ref, dgated_ref)
    cot = jnp.swapaxes(cot_ref[...], 0, 1).reshape(512, 128)
    scaled = jnp.where(lanes_of((512, 128)) == 127, 1.0, scaled_ref[...])
    scaled_t = split(jnp.transpose(scaled))
    for head in range(4):
        param_ref[head * 128 : (head + 1) * 128, :] = dot3(scaled_t, grads[head])
    param_ref[512:640, :] = dot3(jnp.transpose(gated), cot)
    core = place_ref[1]
    keep_ref[...] = param_ref[pl.ds(pl.multiple_of(core * 320, 8), 320), :]
    give_ref[...] = param_ref[pl.ds(pl.multiple_of((1 - core) * 320, 8), 320), :]


def update_kernel(
    factor, got_ref, gate_ref, dgated_ref, wq_ref, wk_ref, wv_ref, wg_ref, wo_ref, update_ref, dnorm_ref
):
    grads, gated = gate_back(got_ref, gate_ref, dgated_ref)
    wq, wk, wv, wg = wq_ref[...], wk_ref[...], wv_ref[...], wg_ref[...]
    update = dot3(gated, wo_ref[...])
    update_ref[...] = jnp.swapaxes(update.reshape(32, 16, 128), 0, 1)
    d_normed = jnp.zeros((512, 128), F32)
    for head in range(4):
        d_normed = d_normed + dot3(grads[head], head_weights(wq, wk, wv, wg, head, factor), NT)
    dnorm_ref[...] = d_normed


def tail_kernel(recv_ref, scaled_ref, send_ref, bias_ref):
    chunk = jnp.sum(recv_ref[:, 0:10, :], axis=0)
    rows = []
    for head in range(4):
        pieces = recv_ref[head, 10:14, :]
        for z in range(1, 8):
            pieces = pieces + recv_ref[z * 4 + head, 10:14, :]
        rows.append(jnp.concatenate([pieces[a : a + 1] for a in range(4)], axis=1))
    bias_t = jnp.concatenate(rows + [jnp.zeros((4, 512), F32)], axis=0)
    bias_ref[...] = bias_t
    bias_w = dot3(bias_t, scaled_ref[...])
    tail = jnp.concatenate([chunk, bias_w[0:4], jnp.zeros((2, 128), F32)], axis=0)
    send_ref[...] = jnp.broadcast_to(tail[None], (8, 16, 128))


def close_kernel(bias_ref, dnorm_ref, scaled_ref, inv_ref, gain_ref, wb_ref, grad_ref):
    scaled = scaled_ref[...]
    wide = jnp.concatenate([bias_ref[...], jnp.zeros((120, 512), F32)], axis=0)
    wb = jnp.concatenate([wb_ref[...], jnp.zeros((124, 128), F32)], axis=0)
    d_normed = dnorm_ref[...] + dot3(jnp.transpose(wide), wb)
    d_scaled = d_normed * gain_ref[...]
    mean_term = jnp.mean(d_scaled, axis=1, keepdims=True)
    cross_term = jnp.mean(d_scaled * scaled, axis=1, keepdims=True)
    d_input = inv_ref[...] * (d_scaled - mean_term - scaled * cross_term)
    grad_ref[...] = jnp.swapaxes(d_input.reshape(32, 16, 128), 0, 1)


def share_kernel(recv_ref, send_ref):
    total = jnp.sum(recv_ref[...], axis=0)
    send_ref[...] = jnp.broadcast_to(total[None], (32, 16, 128))


def finish_kernel(
    factor, count, place_ref, own_ref, other_ref, gain_ref, wq_ref, wk_ref, wv_ref, wg_ref, wb_ref,
    q_ref, k_ref, v_ref, g_ref, shift_ref, o_ref, b_ref, gain_out_ref, own_rows, other_rows,
):
    for at in range(32):
        own_rows[at * 10 : (at + 1) * 10, :] = own_ref[at, 0:10, :]
        other_rows[at * 10 : (at + 1) * 10, :] = other_ref[at, 0:10, :]
    bias_w = jnp.sum(own_ref[:, 10:14, :], axis=0) + jnp.sum(other_ref[:, 10:14, :], axis=0)
    low_half = place_ref[1] == 0
    own_half, other_half = own_rows[...], other_rows[...]
    hold = jnp.concatenate(
        [jnp.where(low_half, own_half, other_half), jnp.where(low_half, other_half, own_half)], axis=0
    )
    wq, wk, wv, wg = wq_ref[...], wk_ref[...], wv_ref[...], wg_ref[...]
    lane = lanes_of((128, 128))
    gain_rows = jnp.transpose(jnp.broadcast_to(gain_ref[...], (128, 128)))
    last = lax.broadcasted_iota(jnp.int32, (128, 128), 0) == 127
    scale = 1.0 / count
    blocks = []
    shift = jnp.zeros((1, 128), F32)
    for head in range(4):
        block = hold[head * 128 : (head + 1) * 128, :]
        sums = turn(block[127:128], 32 * head - 96)
        shift = jnp.where((lane[0:1] >= 32 * head) & (lane[0:1] < 32 * head + 32), sums, shift)
        block = jnp.where(last, 0.0, block)
        blocks.append(jnp.where(last, -jnp.sum(block, axis=0, keepdims=True), block))
    gain_sum = jnp.zeros((128, 128), F32)
    for head in range(4):
        gain_sum = gain_sum + blocks[head] * head_weights(wq, wk, wv, wg, head, factor)
    for ref, group, times in ((q_ref, 0, factor), (k_ref, 1, 1.0), (v_ref, 2, 1.0), (g_ref, 3, 1.0)):
        full = turn(blocks[0], -32 * group)
        for head in range(1, 4):
            full = jnp.where(lane >= 32 * head, turn(blocks[head], 32 * (head - group)), full)
        ref[...] = full * gain_rows * (times * scale)
    o_ref[...] = hold[512:640, :] * scale
    b_ref[...] = bias_w * gain_ref[...] * scale
    shift_ref[...] = shift * scale
    gain_total = jnp.sum(jnp.transpose(gain_sum), axis=0, keepdims=True)
    gain_total = gain_total + jnp.sum(bias_w * wb_ref[...], axis=0, keepdims=True)
    gain_out_ref[...] = gain_total * scale


def cost(us):
    return pl.CostEstimate(flops=int(us * 1e9), bytes_accessed=int(us * 2e6), transcendentals=0)


def call(kernel, out_shape, name, us, vmem=VMEM_BYTES, **extra):
    return pl.pallas_call(
        kernel,
        out_shape=out_shape,
        name=name,
        cost_estimate=cost(us),
        compiler_params=pltpu.CompilerParams(vmem_limit_bytes=vmem),
        **extra,
    )


def shaped(*shape):
    return jax.ShapeDtypeStruct(shape, F32)


def attend_call(place, keep, data, *bias):
    smem, vmem = pl.BlockSpec(memory_space=pltpu.SMEM), pl.BlockSpec(memory_space=pltpu.VMEM)
    return call(
        attend_kernel,
        [shaped(32, 64, 128), shaped(8, 32, 512), shaped(8, 32, 512)],
        "attend",
        12,
        in_specs=[smem] + [vmem] * 6,
        scratch_shapes=[pltpu.VMEM(shape, BF16) for shape in ((256, 768), (256, 256), (128, 256))],
    )(place, keep, data, *bias)


def swap(value, axes):
    return lax.all_to_all(value, axes, 0, 0, tiled=False)


def partner(value, axis, flip):
    return lax.ppermute(value, axis, [(at, at ^ flip) for at in range(lax.axis_size(axis))])


def body(
    pair_rep, cotangent, chain_ids, template, norm_gain, w_query, w_key, w_value, w_gate, gate_bias, w_out, w_bias,
):
    factor = 32 ** (-0.5)
    tokens = chain_ids.shape[0]
    gain = norm_gain.reshape(1, 128)
    square = shaped(128, 128)
    row = shaped(1, 128)

    y, core = lax.axis_index("y"), lax.axis_index("core")
    first = (y * 2 + core) * 32 + lax.axis_index("z") * 4
    place = jnp.stack([y, core, first]).astype(jnp.int32)

    piece, scaled, inverse = call(
        norm_kernel, [shaped(8, 4, 4, 128), shaped(512, 128), shaped(512, 128)], "norm_bias", 1, MOST_VMEM
    )(pair_rep, gain, w_bias)
    vmem = pl.BlockSpec(memory_space=pltpu.VMEM)
    send, gate, d_gated, keep = call(
        lambda *refs: project_kernel(factor, *refs),
        [shaped(8, 4, 64, 128), shaped(512, 128), shaped(512, 128), jax.ShapeDtypeStruct((4, 512), jnp.int32)],
        "project",
        2,
        MOST_VMEM,
        in_specs=[pl.BlockSpec(memory_space=pltpu.SMEM)] + [vmem] * 11,
    )(
        place, scaled, cotangent, gain, w_query, w_key, w_value, w_gate, gate_bias.reshape(1, 128), w_out,
        chain_ids.reshape(1, 512), template,
    )

    piece = swap(piece.reshape(32, 4, 128), ROWS)
    piece, send = lax.optimization_barrier((piece, send))
    data = swap(send.reshape(32, 64, 128), ROWS)
    own = jnp.transpose(piece.reshape(32, 32, 16), (1, 0, 2)).reshape(1, 32, 512)
    near = jnp.concatenate([own, partner(own, "y", 4)], axis=0)
    far = jnp.concatenate([partner(own, "y", 2), partner(own, "y", 6)], axis=0)
    low = jnp.concatenate([near, far], axis=0)
    high = jnp.concatenate([partner(near, "y", 1), partner(far, "y", 1)], axis=0)
    bias = [low, high, partner(low, "core", 1), partner(high, "core", 1)]

    back, d_own, d_other = attend_call(place, keep, data, *bias)

    got = swap(back, ROWS)
    d_bias = d_own + partner(d_other, "core", 1)
    d_bias = d_bias[:4] + partner(d_bias[4:], "y", 1)
    d_bias = d_bias[0] + sum(partner(d_bias[s], "y", flip) for s, flip in ((1, 4), (2, 2), (3, 6)))
    d_bias = jnp.transpose(d_bias.reshape(32, 32, 16), (1, 0, 2)).reshape(32, 4, 128)

    got = got.reshape(8, 4, 64, 128)
    params, give = call(
        param_kernel,
        [shaped(320, 128), shaped(320, 128)],
        "param_grads",
        2,
        in_specs=[pl.BlockSpec(memory_space=pltpu.SMEM)] + [vmem] * 5,
        scratch_shapes=[pltpu.VMEM((640, 128), F32)],
    )(place, got, scaled, gate, d_gated, cotangent)
    update, d_normed = call(
        lambda *refs: update_kernel(factor, *refs), [shaped(16, 32, 128), shaped(512, 128)], "update", 1.5
    )(got, gate, d_gated, w_query, w_key, w_value, w_gate, w_out)

    params = params + partner(give, "core", 1)
    small = swap(jnp.concatenate([params.reshape(32, 10, 128), d_bias], axis=1), ROWS)
    tail, bias_t = call(tail_kernel, [shaped(8, 16, 128), shaped(8, 512)], "tail", 0.5)(small, scaled)
    grad_pair = call(close_kernel, shaped(16, 32, 128), "norm_back", 1)(
        bias_t, d_normed, scaled, inverse, gain, w_bias
    )
    tail = swap(tail, "y")
    tail, update, grad_pair = lax.optimization_barrier((tail, update, grad_pair))
    tail = call(share_kernel, shaped(32, 16, 128), "share", 0.1)(tail)
    tail = swap(tail, ROWS)
    grads = call(
        lambda *refs: finish_kernel(factor, float(tokens), *refs),
        [square, square, square, square, row, square, shaped(4, 128), row],
        "finish",
        1,
        in_specs=[pl.BlockSpec(memory_space=pltpu.SMEM)] + [vmem] * 8,
        scratch_shapes=[pltpu.VMEM((320, 128), F32)] * 2,
    )(place, tail, partner(tail, "core", 1), gain, w_query, w_key, w_value, w_gate, w_bias)
    gq, gk, gv, gg, gshift, go, gb, ggain = grads
    return update, grad_pair, gq, gk, gv, gg, gshift.reshape(128), go, gb, ggain.reshape(128)


def solution(mesh):
    fine = Mesh(mesh.devices.reshape(8, 2, 8, 4), ("y", "core", "z", "x"))
    block = P(ROWS, COLS, None)
    return jax.shard_map(
        body,
        mesh=fine,
        in_specs=(block, block) + (P(),) * 10,
        out_specs=(block, block) + (P(),) * 8,
        check_vma=False,
    )
```

```python
import jax
import jax.numpy as jnp
from jax import lax
from jax.experimental import pallas as pl
from jax.experimental.pallas import tpu as pltpu
from jax.sharding import Mesh, PartitionSpec as P

F32 = jnp.float32
BF16 = jnp.bfloat16
NEG_FILL = -1000000000.0
ROWS = ("z", "x")
COLS = ("y", "core")
VMEM_BYTES = 48 * 1024 * 1024
MOST_VMEM = 60 * 1024 * 1024
NN = (((1,), (0,)), ((), ()))
NT = (((1,), (1,)), ((), ()))


def bdot(left, right, dims=NN):
    return lax.dot_general(left, right, dims, preferred_element_type=F32)


def split(value):
    high = value.astype(BF16)
    return high, (value - high.astype(F32)).astype(BF16)


def dot3(left, right, dims=NN):
    lh, ll = left if isinstance(left, tuple) else split(left)
    rh, rl = right if isinstance(right, tuple) else split(right)
    return bdot(lh, rh, dims) + (bdot(ll, rh, dims) + bdot(lh, rl, dims))


def lanes_of(shape):
    return lax.broadcasted_iota(jnp.int32, shape, 1)


def turn(value, amount):
    amount = amount % value.shape[1]
    return value if amount == 0 else pltpu.roll(value, amount, 1)


def head_weights(wq, wk, wv, wg, head, factor):
    lane = lanes_of(wq.shape)
    at = 32 * head
    out = jnp.where(lane < 32, turn(wq, -at) * factor, turn(wk, 32 - at))
    out = jnp.where(lane < 64, out, turn(wv, 64 - at))
    return jnp.where(lane < 96, out, turn(wg, 96 - at))


def norm_kernel(x_ref, gain_ref, wb_ref, piece_ref, scaled_ref, inv_ref):
    cells = jnp.swapaxes(x_ref[...], 0, 1).reshape(512, 128)
    center = jnp.mean(cells, axis=1, keepdims=True)
    shifted = cells - center
    spread = jnp.mean(shifted * shifted, axis=1, keepdims=True)
    inverse = lax.rsqrt(spread + 1e-05)
    scaled = shifted * inverse
    scaled_ref[...] = scaled
    inv_ref[...] = jnp.broadcast_to(inverse, (512, 128))
    wb = jnp.concatenate([wb_ref[...], jnp.zeros((4, 128), F32)], axis=0)
    bias = dot3(wb, scaled * gain_ref[...], NT)
    for head in range(4):
        for part in range(4):
            row = bias[head : head + 1, part * 128 : (part + 1) * 128]
            piece_ref[:, head, part, :] = jnp.broadcast_to(row, (8, 128))


def project_kernel(
    factor, place_ref, scaled_ref, cot_ref, gain_ref, wq_ref, wk_ref, wv_ref, wg_ref, gb_ref, wo_ref,
    chain_ref, template_ref, send_ref, gate_ref, dgated_ref, keep_ref,
):
    cot = jnp.swapaxes(cot_ref[...], 0, 1).reshape(512, 128)
    normed = split(scaled_ref[...] * gain_ref[...])
    wq, wk, wv, wg = wq_ref[...], wk_ref[...], wv_ref[...], wg_ref[...]
    gate = jax.nn.sigmoid(dot3(normed, wg) + gb_ref[...])
    d_gated = dot3(cot, wo_ref[...], NT)
    gate_ref[...] = gate
    dgated_ref[...] = d_gated
    d_att = d_gated * gate
    lane = lanes_of((512, 128))
    for head in range(4):
        weights = head_weights(wq, wk, wv, wg, head, factor)
        block = jnp.where(lane < 96, dot3(normed, weights), turn(d_att, 96 - 32 * head))
        send_ref[:, head] = block.reshape(8, 64, 128)
    first = place_ref[2]
    chain = chain_ref[...]
    token = lanes_of((1, 512))
    near = lanes_of((8, 8)) == first // 64
    blocks = jnp.max(jnp.where(near, template_ref[...], 0), axis=1, keepdims=True)
    open_block = jnp.zeros((1, 512), jnp.int32)
    for block in range(8):
        open_block = jnp.where(token // 64 == block, blocks[block : block + 1], open_block)
    for column in range(4):
        own = jnp.max(jnp.where(token == first + column, chain, 0), axis=1, keepdims=True)
        keep_ref[column : column + 1, :] = jnp.where(chain == own, 1, open_block)


def picker(groups):
    shape = (256, 128)
    source, lane = lax.broadcasted_iota(jnp.int32, shape, 0), lanes_of(shape)
    wanted = jnp.full(shape, -1, jnp.int32)
    for group, pick in enumerate(groups):
        if pick is not None:
            wanted = jnp.where(lane // 32 == group, pick[0] * 128 + pick[1] * 32 + lane % 32, wanted)
    return jnp.where(source == wanted, 1.0, 0.0)


def left(group):
    return [(0, group), (1, group), (0, group), (1, group)]


def right(group):
    return [(0, group), (0, group), (1, group), (1, group)]


def fill_pickers(keys_ref, rows_ref, turns_ref):
    keys = [
        right(1),
        right(2),
        [(0, 1), (1, 1), None, None],
        [(0, 1), None, None, None],
        [None, None, (1, 2), (0, 2)],
        [None, None, None, (0, 2)],
    ]
    for at, groups in enumerate(keys):
        keys_ref[:, at * 128 : (at + 1) * 128] = picker(groups).astype(BF16)
    for at, group in enumerate((0, 3)):
        pick = picker(left(group))
        rows_ref[:, at * 128 : (at + 1) * 128] = pick.astype(BF16)
        turns_ref[at * 64 : (at + 1) * 64, :] = jnp.transpose(pick)[0:64].astype(BF16)


def halves_of(value):
    high = value.astype(BF16)
    return jnp.concatenate([high, (value - high.astype(F32)).astype(BF16)], axis=1)


def attend_kernel(
    place_ref, keep_ref, data_ref, own_low_ref, own_high_ref, other_low_ref, other_high_ref,
    out_ref, d_own_ref, d_other_ref,
    keys_ref, rows_ref, turns_ref,
):
    y, core = place_ref[0], place_ref[1]
    fill_pickers(keys_ref, rows_ref, turns_ref)
    chunk_rows = 256
    per = chunk_rows // 32
    sub = lanes_of((chunk_rows, 128))
    chunks = []
    sides = (((own_low_ref, own_high_ref), d_own_ref), ((other_low_ref, other_high_ref), d_other_ref))
    for side, (bias_refs, db_ref) in enumerate(sides):
        half = core if side == 0 else 1 - core
        for s0 in range(0, 8, per):
            starts = [(y ^ ((s >> 2) | (s & 2) | ((s & 1) << 2))) * 4 + half * 2 for s in range(s0, s0 + per)]
            chunks.append((starts, bias_refs, db_ref, s0))

    def column_keys(column):
        here = pl.ds(column * 16, 16)
        picked = bdot(halves_of(data_ref[:, here].reshape(512, 128)), keys_ref[...]).astype(BF16)
        return [picked[:, at * 128 : (at + 1) * 128] for at in range(6)] + [keep_ref[column : column + 1, :] > 0]

    def first(column, keys, chunk):
        k_right, v_right, k_both, k_first, v_both, v_first, keep = keys
        starts, bias_refs, db_ref, s0 = chunk
        here = pl.ds(column * 16, 16)
        rows = jnp.concatenate([data_ref[pl.ds(start, 2), here].reshape(32, 128) for start in starts], axis=0)
        both = halves_of(rows)
        q_left = bdot(both, rows_ref[:, 0:128]).astype(BF16)
        q_t = bdot(turns_ref[0:64], both, NT).astype(BF16)
        bias = jnp.concatenate([ref[...].reshape(128, 512) for ref in bias_refs], axis=0)
        scores = bdot(q_left, k_right, NT) + bias
        return rows, q_t, jnp.where(keep, scores, NEG_FILL)

    def second(keys, state):
        k_right, v_right, k_both, k_first, v_both, v_first, keep = keys
        rows, q_t, scores = state
        highest = jnp.max(scores, axis=1, keepdims=True)
        weights = jnp.exp(scores - highest)
        inv_total = 1.0 / jnp.sum(weights, axis=1, keepdims=True)
        wh, wl = split(weights)
        output = bdot(wh, v_both) + bdot(wl, v_first)
        output = (output + pltpu.roll(output, 32, 1)) * inv_total
        d_out = jnp.where(sub >= 96, rows, 0.0) * inv_total
        centred = jnp.sum(d_out * output, axis=1, keepdims=True)
        d_both = halves_of(d_out)
        d_left = bdot(d_both, rows_ref[:, 128:256]).astype(BF16)
        d_weights = bdot(d_left, v_right, NT)
        d_t = bdot(turns_ref[64:128], d_both, NT).astype(BF16)
        return weights, output, d_weights, centred, (d_t, wh, wl), q_t

    def third(column, keys, chunk, state):
        k_right, v_right, k_both, k_first, v_both, v_first, keep = keys
        starts, bias_refs, db_ref, s0 = chunk
        weights, output, d_weights, centred, (d_t, wh, wl), q_t = state
        both = bdot(d_t, wh)
        dv_t = both[0:32] + both[32:64] + bdot(d_t[0:32], wl)
        d_scores = weights * (d_weights - centred)
        for slot in range(8):
            piece = d_scores[slot * 32 : (slot + 1) * 32]
            at = (slot & 3) * 2 + (slot >> 2)
            db_ref[at] = piece if column == 0 else db_ref[at] + piece
        sh, sl = split(d_scores)
        d_query = bdot(sh, k_both) + bdot(sl, k_first)
        d_query = d_query + pltpu.roll(d_query, 96, 1)
        both = bdot(q_t, sh)
        dk_t = both[0:32] + both[32:64] + bdot(q_t[0:32], sl)
        return jnp.where(sub < 32, d_query, output), dk_t, dv_t

    mixed = (sub >= 32) & (sub < 96)

    def finish(column, done):
        here = pl.ds(column * 16, 16)
        zeros = jnp.zeros((32, 512), F32)
        dk_t = sum(part[1] for part in done)
        dv_t = sum(part[2] for part in done)
        result = jnp.transpose(jnp.concatenate([zeros, dk_t, dv_t, zeros], axis=0))
        out_ref[:, here] = result.reshape(32, 16, 128)
        for (starts, _, _, _), part in zip(chunks, done):
            held = jnp.concatenate([out_ref[pl.ds(start, 2), here].reshape(32, 128) for start in starts], axis=0)
            value = jnp.where(mixed, held, part[0])
            for s, start in enumerate(starts):
                out_ref[pl.ds(start, 2), here] = value[s * 32 : (s + 1) * 32].reshape(2, 16, 128)

    work = [(column, chunk) for column in range(4) for chunk in chunks]
    keys, ones, twos, dones = {}, {}, {}, {}
    for step in range(len(work) + 2):
        if step < len(work):
            column, chunk = work[step]
            if column not in keys:
                keys[column] = column_keys(column)
            ones[step] = first(column, keys[column], chunk)
        if 0 <= step - 1 < len(work):
            twos[step - 1] = second(keys[work[step - 1][0]], ones.pop(step - 1))
        if 0 <= step - 2 < len(work):
            column, chunk = work[step - 2]
            dones.setdefault(column, []).append(third(column, keys[column], chunk, twos.pop(step - 2)))
            if len(dones[column]) == len(chunks):
                finish(column, dones.pop(column))


def gate_back(got_ref, gate_ref, dgated_ref):
    lane = lanes_of((512, 128))
    gate = gate_ref[...]
    got = [got_ref[:, head].reshape(512, 128) for head in range(4)]
    att = got[3]
    for head in range(3):
        moved = turn(got[head], 32 * head - 96)
        att = jnp.where((lane >= 32 * head) & (lane < 32 * head + 32), moved, att)
    d_pre = dgated_ref[...] * att * gate * (1.0 - gate)
    grads = [jnp.where(lane < 96, got[head], turn(d_pre, 96 - 32 * head)) for head in range(4)]
    return grads, gate * att


def param_kernel(place_ref, got_ref, scaled_ref, gate_ref, dgated_ref, cot_ref, keep_ref, give_ref, param_ref):
    grads, gated = gate_back(got_ref, gate_ref, dgated_ref)
    cot = jnp.swapaxes(cot_ref[...], 0, 1).reshape(512, 128)
    scaled = jnp.where(lanes_of((512, 128)) == 127, 1.0, scaled_ref[...])
    scaled_t = split(jnp.transpose(scaled))
    for head in range(4):
        param_ref[head * 128 : (head + 1) * 128, :] = dot3(scaled_t, grads[head])
    param_ref[512:640, :] = dot3(jnp.transpose(gated), cot)
    core = place_ref[1]
    keep_ref[...] = param_ref[pl.ds(pl.multiple_of(core * 320, 8), 320), :]
    give_ref[...] = param_ref[pl.ds(pl.multiple_of((1 - core) * 320, 8), 320), :]


def update_kernel(
    factor, got_ref, gate_ref, dgated_ref, wq_ref, wk_ref, wv_ref, wg_ref, wo_ref, update_ref, dnorm_ref
):
    grads, gated = gate_back(got_ref, gate_ref, dgated_ref)
    wq, wk, wv, wg = wq_ref[...], wk_ref[...], wv_ref[...], wg_ref[...]
    update = dot3(gated, wo_ref[...])
    update_ref[...] = jnp.swapaxes(update.reshape(32, 16, 128), 0, 1)
    d_normed = jnp.zeros((512, 128), F32)
    for head in range(4):
        d_normed = d_normed + dot3(grads[head], head_weights(wq, wk, wv, wg, head, factor), NT)
    dnorm_ref[...] = d_normed


def tail_kernel(recv_ref, scaled_ref, send_ref, bias_ref):
    chunk = jnp.sum(recv_ref[:, 0:10, :], axis=0)
    rows = []
    for head in range(4):
        pieces = recv_ref[head, 10:14, :]
        for z in range(1, 8):
            pieces = pieces + recv_ref[z * 4 + head, 10:14, :]
        rows.append(jnp.concatenate([pieces[a : a + 1] for a in range(4)], axis=1))
    bias_t = jnp.concatenate(rows + [jnp.zeros((4, 512), F32)], axis=0)
    bias_ref[...] = bias_t
    bias_w = dot3(bias_t, scaled_ref[...])
    tail = jnp.concatenate([chunk, bias_w[0:4], jnp.zeros((2, 128), F32)], axis=0)
    send_ref[...] = jnp.broadcast_to(tail[None], (8, 16, 128))


def close_kernel(bias_ref, dnorm_ref, scaled_ref, inv_ref, gain_ref, wb_ref, grad_ref):
    scaled = scaled_ref[...]
    wide = jnp.concatenate([bias_ref[...], jnp.zeros((120, 512), F32)], axis=0)
    wb = jnp.concatenate([wb_ref[...], jnp.zeros((124, 128), F32)], axis=0)
    d_normed = dnorm_ref[...] + dot3(jnp.transpose(wide), wb)
    d_scaled = d_normed * gain_ref[...]
    mean_term = jnp.mean(d_scaled, axis=1, keepdims=True)
    cross_term = jnp.mean(d_scaled * scaled, axis=1, keepdims=True)
    d_input = inv_ref[...] * (d_scaled - mean_term - scaled * cross_term)
    grad_ref[...] = jnp.swapaxes(d_input.reshape(32, 16, 128), 0, 1)


def share_kernel(recv_ref, send_ref):
    total = jnp.sum(recv_ref[...], axis=0)
    send_ref[...] = jnp.broadcast_to(total[None], (32, 16, 128))


def finish_kernel(
    factor, count, place_ref, own_ref, other_ref, gain_ref, wq_ref, wk_ref, wv_ref, wg_ref, wb_ref,
    q_ref, k_ref, v_ref, g_ref, shift_ref, o_ref, b_ref, gain_out_ref, own_rows, other_rows,
):
    for at in range(32):
        own_rows[at * 10 : (at + 1) * 10, :] = own_ref[at, 0:10, :]
        other_rows[at * 10 : (at + 1) * 10, :] = other_ref[at, 0:10, :]
    bias_w = jnp.sum(own_ref[:, 10:14, :], axis=0) + jnp.sum(other_ref[:, 10:14, :], axis=0)
    low_half = place_ref[1] == 0
    own_half, other_half = own_rows[...], other_rows[...]
    hold = jnp.concatenate(
        [jnp.where(low_half, own_half, other_half), jnp.where(low_half, other_half, own_half)], axis=0
    )
    wq, wk, wv, wg = wq_ref[...], wk_ref[...], wv_ref[...], wg_ref[...]
    lane = lanes_of((128, 128))
    gain_rows = jnp.transpose(jnp.broadcast_to(gain_ref[...], (128, 128)))
    last = lax.broadcasted_iota(jnp.int32, (128, 128), 0) == 127
    scale = 1.0 / count
    blocks = []
    shift = jnp.zeros((1, 128), F32)
    for head in range(4):
        block = hold[head * 128 : (head + 1) * 128, :]
        sums = turn(block[127:128], 32 * head - 96)
        shift = jnp.where((lane[0:1] >= 32 * head) & (lane[0:1] < 32 * head + 32), sums, shift)
        block = jnp.where(last, 0.0, block)
        blocks.append(jnp.where(last, -jnp.sum(block, axis=0, keepdims=True), block))
    gain_sum = jnp.zeros((128, 128), F32)
    for head in range(4):
        gain_sum = gain_sum + blocks[head] * head_weights(wq, wk, wv, wg, head, factor)
    for ref, group, times in ((q_ref, 0, factor), (k_ref, 1, 1.0), (v_ref, 2, 1.0), (g_ref, 3, 1.0)):
        full = turn(blocks[0], -32 * group)
        for head in range(1, 4):
            full = jnp.where(lane >= 32 * head, turn(blocks[head], 32 * (head - group)), full)
        ref[...] = full * gain_rows * (times * scale)
    o_ref[...] = hold[512:640, :] * scale
    b_ref[...] = bias_w * gain_ref[...] * scale
    shift_ref[...] = shift * scale
    gain_total = jnp.sum(jnp.transpose(gain_sum), axis=0, keepdims=True)
    gain_total = gain_total + jnp.sum(bias_w * wb_ref[...], axis=0, keepdims=True)
    gain_out_ref[...] = gain_total * scale


def cost(us):
    return pl.CostEstimate(flops=int(us * 1e9), bytes_accessed=int(us * 2e6), transcendentals=0)


def call(kernel, out_shape, name, us, vmem=VMEM_BYTES, **extra):
    return pl.pallas_call(
        kernel,
        out_shape=out_shape,
        name=name,
        cost_estimate=cost(us),
        compiler_params=pltpu.CompilerParams(vmem_limit_bytes=vmem),
        **extra,
    )


def shaped(*shape):
    return jax.ShapeDtypeStruct(shape, F32)


def attend_call(place, keep, data, *bias):
    smem, vmem = pl.BlockSpec(memory_space=pltpu.SMEM), pl.BlockSpec(memory_space=pltpu.VMEM)
    return call(
        attend_kernel,
        [shaped(32, 64, 128), shaped(8, 32, 512), shaped(8, 32, 512)],
        "attend",
        12,
        in_specs=[smem] + [vmem] * 6,
        scratch_shapes=[pltpu.VMEM(shape, BF16) for shape in ((256, 768), (256, 256), (128, 256))],
    )(place, keep, data, *bias)


def swap(value, axes):
    return lax.all_to_all(value, axes, 0, 0, tiled=False)


def partner(value, axis, flip):
    return lax.ppermute(value, axis, [(at, at ^ flip) for at in range(lax.axis_size(axis))])


def body(
    pair_rep, cotangent, chain_ids, template, norm_gain, w_query, w_key, w_value, w_gate, gate_bias, w_out, w_bias,
):
    factor = 32 ** (-0.5)
    tokens = chain_ids.shape[0]
    gain = norm_gain.reshape(1, 128)
    square = shaped(128, 128)
    row = shaped(1, 128)

    y, core = lax.axis_index("y"), lax.axis_index("core")
    first = (y * 2 + core) * 32 + lax.axis_index("z") * 4
    place = jnp.stack([y, core, first]).astype(jnp.int32)

    piece, scaled, inverse = call(
        norm_kernel, [shaped(8, 4, 4, 128), shaped(512, 128), shaped(512, 128)], "norm_bias", 1, MOST_VMEM
    )(pair_rep, gain, w_bias)
    vmem = pl.BlockSpec(memory_space=pltpu.VMEM)
    send, gate, d_gated, keep = call(
        lambda *refs: project_kernel(factor, *refs),
        [shaped(8, 4, 64, 128), shaped(512, 128), shaped(512, 128), jax.ShapeDtypeStruct((4, 512), jnp.int32)],
        "project",
        2,
        MOST_VMEM,
        in_specs=[pl.BlockSpec(memory_space=pltpu.SMEM)] + [vmem] * 11,
    )(
        place, scaled, cotangent, gain, w_query, w_key, w_value, w_gate, gate_bias.reshape(1, 128), w_out,
        chain_ids.reshape(1, 512), template,
    )

    piece = swap(piece.reshape(32, 4, 128), ROWS)
    piece, send = lax.optimization_barrier((piece, send))
    data = swap(send.reshape(32, 64, 128), ROWS)
    own = jnp.transpose(piece.reshape(32, 32, 16), (1, 0, 2)).reshape(1, 32, 512)
    near = jnp.concatenate([own, partner(own, "y", 4)], axis=0)
    far = jnp.concatenate([partner(own, "y", 2), partner(own, "y", 6)], axis=0)
    low = jnp.concatenate([near, far], axis=0)
    high = jnp.concatenate([partner(near, "y", 1), partner(far, "y", 1)], axis=0)
    bias = [low, high, partner(low, "core", 1), partner(high, "core", 1)]

    back, d_own, d_other = attend_call(place, keep, data, *bias)

    got = swap(back, ROWS)
    far = d_own[2:8] + partner(d_other[2:8], "core", 1)
    pairs = d_own[0:2] + partner(d_other[0:2], "core", 1)
    for at, flip in ((0, 4), (2, 2), (4, 6)):
        pairs = pairs + partner(far[at : at + 2], "y", flip)
    d_bias = pairs[0] + partner(pairs[1], "y", 1)
    d_bias = jnp.transpose(d_bias.reshape(32, 32, 16), (1, 0, 2)).reshape(32, 4, 128)

    got = got.reshape(8, 4, 64, 128)
    params, give = call(
        param_kernel,
        [shaped(320, 128), shaped(320, 128)],
        "param_grads",
        2,
        in_specs=[pl.BlockSpec(memory_space=pltpu.SMEM)] + [vmem] * 5,
        scratch_shapes=[pltpu.VMEM((640, 128), F32)],
    )(place, got, scaled, gate, d_gated, cotangent)
    update, d_normed = call(
        lambda *refs: update_kernel(factor, *refs), [shaped(16, 32, 128), shaped(512, 128)], "update", 1.5
    )(got, gate, d_gated, w_query, w_key, w_value, w_gate, w_out)

    params = params + partner(give, "core", 1)
    small = swap(jnp.concatenate([params.reshape(32, 10, 128), d_bias], axis=1), ROWS)
    tail, bias_t = call(tail_kernel, [shaped(8, 16, 128), shaped(8, 512)], "tail", 0.5)(small, scaled)
    grad_pair = call(close_kernel, shaped(16, 32, 128), "norm_back", 1)(
        bias_t, d_normed, scaled, inverse, gain, w_bias
    )
    tail = swap(tail, "y")
    tail, update, grad_pair = lax.optimization_barrier((tail, update, grad_pair))
    tail = call(share_kernel, shaped(32, 16, 128), "share", 0.1)(tail)
    tail = swap(tail, ROWS)
    grads = call(
        lambda *refs: finish_kernel(factor, float(tokens), *refs),
        [square, square, square, square, row, square, shaped(4, 128), row],
        "finish",
        1,
        in_specs=[pl.BlockSpec(memory_space=pltpu.SMEM)] + [vmem] * 8,
        scratch_shapes=[pltpu.VMEM((320, 128), F32)] * 2,
    )(place, tail, partner(tail, "core", 1), gain, w_query, w_key, w_value, w_gate, w_bias)
    gq, gk, gv, gg, gshift, go, gb, ggain = grads
    return update, grad_pair, gq, gk, gv, gg, gshift.reshape(128), go, gb, ggain.reshape(128)


def solution(mesh):
    fine = Mesh(mesh.devices.reshape(8, 2, 8, 4), ("y", "core", "z", "x"))
    block = P(ROWS, COLS, None)
    return jax.shard_map(
        body,
        mesh=fine,
        in_specs=(block, block) + (P(),) * 10,
        out_specs=(block, block) + (P(),) * 8,
        check_vma=False,
    )
```
